32 devices in a mesh: groups: 2 (over y), patch: 8 (over z, x), visit: 2 (over core).
Axes of the slice: x: 2, y: 2, z: 4, core: 2. Of those that a mesh axis runs over, the one named last changes fastest.
Arguments:
- visit_tiles: bfloat16 [1792, 64, 1024], P(('groups', 'patch', 'visit')), parts along dimension 0, may hold values from -6 to 6
- tile_patch: int32 [1792], P(('groups', 'patch', 'visit')), parts along dimension 0, may hold values from 0 to 7, as said below
- offsets: int32 [1792, 2], P(('groups', 'patch', 'visit')), parts along dimension 0, may hold values from -128 to 127
- psf_coefs: int32 [1792, 3], P(('groups', 'patch', 'visit')), parts along dimension 0, may hold values from 16 to 80
- weights: bfloat16 [1792], P(('groups', 'patch', 'visit')), parts along dimension 0, may hold values from 0.19921875 to 4
Outputs:
- coadd: float32 [1024, 1024], P(('groups', 'patch')), parts along dimension 0
- detection: float32 [1024, 1024], P(('groups', 'patch')), parts along dimension 0
The draws below stay inside these ranges and needn't reach their ends.
There are 2 independent parts, one for each index of `groups`. The reference program is written for one: setup_inputs(seed, part) draws one part's arguments, and reference() takes and returns one part's arrays. A program takes and returns all parts, laid end to end along the dimension named above; each array names one. Nothing has to cross between parts.
Inputs may be any that keep to these rules, and one draw needn't show every extreme that they name: `tile_patch`: among the 56 tiles of one device at most 14 name any one patch; 2 deep-field patches are named by exactly 14 tiles of every device; every patch is named by some tile.
All inputs are finite; a program needn't handle non-finite values.
Results may differ from the reference program's by a relative error of at most 0.0048.
Values may be sent and summed in bfloat16 or wider, within the bound.
A program may use at most 128 MiB of HBM per device.

```python
import math
import jax
import jax.numpy as jnp
from jax import lax

PH = 64
PW = 1024
TILES_DEV = 56
HALO = 8
DEEP = 2
PATCHES = 8
CAP = 14
TILES = 896


def draw_tile_patch(key, part):
    block_count = TILES // TILES_DEV
    slot_total = PATCHES * CAP
    deep_patches = jax.random.permutation(jax.random.fold_in(key, 7), PATCHES)[:DEEP].astype(jnp.int32)
    slot_patch = jnp.arange(slot_total, dtype=jnp.int32) // CAP
    slot_within = jnp.arange(slot_total, dtype=jnp.int32) % CAP
    is_deep = jnp.any(slot_patch[:, None] == deep_patches[None, :], axis=1)

    def one_block(block_key, block_index):
        first_key, second_key = jax.random.split(block_key)
        order_rank = jax.random.permutation(first_key, slot_total).astype(jnp.int32)
        covered = (slot_patch == block_index % PATCHES) & (slot_within == 0)
        priority = jnp.where(is_deep | covered, -1, order_rank)
        chosen = jnp.argsort(priority, stable=True)[:TILES_DEV]
        picked = slot_patch[chosen]
        return picked[jax.random.permutation(second_key, TILES_DEV)]
    block_keys = jax.random.split(jax.random.fold_in(key, 11), block_count)
    block_ids = jnp.arange(block_count, dtype=jnp.int32)
    return jax.vmap(one_block)(block_keys, block_ids).reshape(-1).astype(jnp.int32)


def set_ends(drawn, own_key, least, top_value):
    spot = [jax.random.randint(jax.random.fold_in(own_key, axis), (), 0, length) for axis, length in enumerate(drawn.shape)]
    main_axis = drawn.shape.index(max(drawn.shape))
    neighbour = spot[:main_axis] + [(spot[main_axis] + 1) % drawn.shape[main_axis]] + spot[main_axis + 1:]
    return drawn.at[tuple(spot)].set(least).at[tuple(neighbour)].set(top_value)


def shard_levels(rng, shape, pieces, smallest, high):
    factor_of = 1.0
    for dim, parts in pieces:
        draws = jax.random.uniform(jax.random.fold_in(jax.random.fold_in(rng, 6), dim), (parts,), jnp.float32, smallest / len(pieces), high / len(pieces))
        factor_of = factor_of * jnp.repeat(jnp.exp(draws), shape[dim] // parts).reshape((-1,) + (1,) * (len(shape) - 1 - dim))
    return factor_of


def bell_draw(stream_key, dims, scale, limit, cuts=(), kind=jnp.bfloat16):
    array = jax.random.normal(stream_key, dims, jnp.float32) * scale
    if len(cuts) > 0:
        array = shard_levels(stream_key, dims, cuts, -0.22, 0.18) * array
    return jnp.clip(array, min=-limit, max=limit).astype(kind)


def setup_inputs(seed: int = 0, part: int = 0) -> dict:
    splits = jax.random.split(jax.random.key(seed), 6)
    part_keys = jax.random.split(jax.random.fold_in(splits[5], part), 6)
    return {
        "visit_tiles": bell_draw(part_keys[0], (TILES, PH, PW), 1.0, 6.0, ((0, 16),)),
        "tile_patch": draw_tile_patch(jax.random.fold_in(jax.random.fold_in(splits[5], part), 71), part),
        "offsets": set_ends(jax.random.randint(part_keys[2], (TILES, 2), -128, 128), jax.random.fold_in(part_keys[2], 1), -128, 127).astype(jnp.int32),
        "psf_coefs": set_ends(jax.random.randint(part_keys[3], (TILES, 3), 16, 81), jax.random.fold_in(part_keys[3], 1), 16, 80).astype(jnp.int32),
        "weights": jnp.clip(jnp.exp(math.log(4.0) - 2.9996462 * jax.random.uniform(part_keys[4], (TILES,), jnp.float32) ** shard_levels(part_keys[4], (TILES,), ((0, 16),), -0.2, 0.2)), 0.19921875, 4.0).astype(jnp.bfloat16),
    }


PSF_SIGMAS = (0.75, 1.5, 3.0)
psf_reach = 16

def lanczos(value):
    inside = jnp.abs(value) < 3.0
    return jnp.where(inside, jnp.sinc(value) * jnp.sinc(value / 3.0), 0.0)

def gaussian(distance, sigma, reach):
    shape = jnp.exp(-distance * distance / (2.0 * sigma * sigma)) / (math.pi * sigma * sigma) ** 0.25
    return jnp.where(jnp.abs(distance) <= reach, shape, 0.0)

def shift_axis(image, offset, axis):
    whole_shift = offset // 64
    frac_shift = (offset - 64 * whole_shift).astype(jnp.float32) / 64.0
    length = image.shape[axis]
    widths = [(0, 0), (0, 0)]
    widths[axis] = (5, 5)
    padded = jnp.pad(image, widths)
    running = jnp.zeros(image.shape, jnp.float32)
    for tap_index in range(-2, 4):
        tap_weight = lanczos(frac_shift - tap_index).astype(jnp.bfloat16).astype(jnp.float32)
        start = (5 + whole_shift + tap_index).astype(jnp.int32)
        piece = lax.dynamic_slice_in_dim(padded, start, length, axis)
        running = running + tap_weight * piece.astype(jnp.float32)
    return running.astype(jnp.bfloat16)

def warp_ref(tile, offset):
    shifted = shift_axis(tile, offset[0], 0)
    return shift_axis(shifted, offset[1], 1)

def apply_taps(field, axis, sigma, reach):
    length = field.shape[axis]
    widths = [(0, 0)] * field.ndim
    widths[axis] = (reach, reach)
    padded = jnp.pad(field, widths)
    running = jnp.zeros(field.shape, jnp.float32)
    for distance in range(-reach, reach + 1):
        coeff = gaussian(jnp.float32(distance), sigma, reach)
        piece = lax.slice_in_dim(padded, reach - distance, reach - distance + length, axis=axis)
        running = running + coeff * piece
    return running

def reference(visit_tiles, tile_patch, offsets, psf_coefs, weights):
    block_count = TILES // TILES_DEV
    blocks = (visit_tiles.reshape(block_count, TILES_DEV, PH, PW), tile_patch.reshape(block_count, TILES_DEV), offsets.reshape(block_count, TILES_DEV, 2), psf_coefs.reshape(block_count, TILES_DEV, 3), weights.reshape(block_count, TILES_DEV))

    def accumulate(carry, block):
        stacks, weight_sq = carry
        tiles_blk, patch_blk, offset_blk, coef_blk, weight_blk = block
        warped = jax.vmap(warp_ref)(tiles_blk, offset_blk)
        weight_f = weight_blk.astype(jnp.float32)
        factor = weight_f[:, None] * (coef_blk.astype(jnp.float32) / 64.0)
        contrib = factor[:, :, None, None] * warped.astype(jnp.float32)[:, None]
        stacks = stacks.at[patch_blk].add(contrib)
        weight_sq = weight_sq.at[patch_blk].add(weight_f * weight_f)
        return ((stacks, weight_sq), None)
    start = (jnp.zeros((PATCHES, 3, PH, PW), jnp.float32), jnp.zeros((PATCHES,), jnp.float32))
    (stacks, weight_sq), _ = lax.scan(accumulate, start, blocks)
    matched = jnp.zeros((PATCHES, PH, PW), jnp.float32)
    for basis in range(3):
        sigma = PSF_SIGMAS[basis]
        blurred = apply_taps(stacks[:, basis], 1, sigma, psf_reach)
        matched = matched + apply_taps(blurred, 2, sigma, psf_reach)
    coadd = (matched / jnp.sqrt(weight_sq)[:, None, None]).reshape(PATCHES * PH, PW)
    detect_sigma = HALO / 4.0
    detection = apply_taps(apply_taps(coadd, 0, detect_sigma, HALO), 1, detect_sigma, HALO)
    return (coadd, detection)
```

```python
import functools
import math

import jax
import jax.numpy as jnp
import numpy as np
from jax import lax
from jax.experimental import pallas as pl
from jax.experimental.pallas import tpu as pltpu
from jax.sharding import PartitionSpec as P

HALO = 8
PSF_SIGMAS = (0.75, 1.5, 3.0)
PSF_REACH = 16
TAPS = 11
MID = TAPS // 2
LANES = 128
HALF = 64
MESH = pl.DeviceIdType.MESH
BF16 = jnp.bfloat16
F32 = jnp.float32


def gaussian(distance, sigma, reach):
    distance = np.asarray(distance, np.float32)
    shape = np.exp(-distance * distance / (2.0 * sigma * sigma)) / (math.pi * sigma * sigma) ** 0.25
    return np.where(np.abs(distance) <= reach, shape, 0.0).astype(np.float32)


def split_high_low(matrix):
    high = jnp.asarray(matrix).astype(BF16)
    return high, (jnp.asarray(matrix) - high.astype(F32)).astype(BF16)


def lanczos(value):
    inside = jnp.abs(value) < 3.0
    return jnp.where(inside, jnp.sinc(value) * jnp.sinc(value / 3.0), 0.0)


def column_warp(tile, col_taps, v):
    rows, cols = tile.shape
    low, high = HALF - 16, HALF + LANES + 16
    shape = (high - low, LANES)
    distance = HALF - low + lax.broadcasted_iota(jnp.int32, shape, 1) - lax.broadcasted_iota(jnp.int32, shape, 0)
    band = jnp.zeros(shape, F32)
    for t in range(TAPS):
        band = jnp.where(distance == t - MID, col_taps[v * TAPS + t], band)
    band = band.astype(BF16)
    matrix = jnp.concatenate([jnp.zeros((low, LANES), BF16), band, jnp.zeros((2 * LANES - high, LANES), BF16)], axis=0)
    edge = jnp.zeros((rows, LANES), BF16)
    padded = jnp.concatenate([edge, tile, edge], axis=1)
    blocks = cols // LANES + 1
    windows = jnp.concatenate([padded[:, m * LANES : (m + 2) * LANES] for m in range(blocks)], axis=0)
    return jnp.dot(windows, matrix, preferred_element_type=F32).astype(BF16)


def row_matrices(meta, g_high, g_low, rows):
    depth = meta.shape[1]
    shape = (rows, depth)
    distance = lax.broadcasted_iota(jnp.int32, shape, 0) - lax.broadcasted_iota(jnp.int32, shape, 1) % rows
    shift = jnp.zeros(shape, F32)
    for t in range(TAPS):
        shift = jnp.where(distance == t - MID, jnp.broadcast_to(meta[t : t + 1, :], shape), shift)
    shift = shift.astype(BF16)
    blurred = jnp.dot(g_high, shift, preferred_element_type=F32) + jnp.dot(g_low, shift, preferred_element_type=F32)
    pieces = []
    for k in range(3):
        factor = meta[TAPS + k : TAPS + k + 1, :] + meta[TAPS + 3 + k : TAPS + 4 + k, :]
        pieces.append(blurred[k * rows : (k + 1) * rows] * factor)
    return jnp.concatenate(pieces, axis=0).astype(BF16)


def stack_kernel(
    owners, capacity, chunk, source, col_taps, tiles_hbm, meta_ref, g_high, g_low, g_cols, out_ref, tiles, warped, blur, sems
):
    count, rows, cols = tiles.shape
    wide = cols + LANES
    chunks = count // chunk

    def load(c):
        part = pl.ds(c * chunk, chunk)
        return pltpu.make_async_copy(tiles_hbm.at[part], tiles.at[part], sems.at[c])

    for c in range(chunks):
        load(c).start()
    for c in range(chunks):
        load(c).wait()

        def warp(step, carry):
            v = c * chunk + step
            result = column_warp(tiles[v], col_taps, v)
            for m in range(wide // LANES):
                warped[v, :, m * LANES : (m + 1) * LANES] = result[m * rows : (m + 1) * rows]
            return carry

        lax.fori_loop(0, chunk, warp, 0, unroll=True if chunk <= 4 else 4)

    depth = capacity * rows
    pieces = [(a, min(a + 3 * LANES, wide)) for a in range(0, wide, 3 * LANES)]

    def patch(p, carry):
        meta = meta_ref[:, pl.ds(pl.multiple_of(p * depth, LANES), depth)]
        left = row_matrices(meta, g_high[...], g_low[...], rows)
        slots = [source[p * capacity + r] for r in range(capacity)]
        for a, b in pieces:
            right = jnp.concatenate([warped[s, :, a:b] for s in slots], axis=0)
            total = jnp.dot(left, right, preferred_element_type=F32)
            lane = a + lax.broadcasted_iota(jnp.int32, total.shape, 1)
            if a < HALF or b > wide - HALF:
                total = jnp.where((lane >= HALF) & (lane < wide - HALF), total, 0.0)
            blur[:, a:b] = total.astype(BF16)
        windows = jnp.concatenate(
            [
                jnp.concatenate([blur[k * rows : (k + 1) * rows, m * LANES : (m + 2) * LANES] for k in range(3)], axis=1)
                for m in range(cols // LANES)
            ],
            axis=0,
        )
        result = jnp.dot(windows, g_cols[...], preferred_element_type=F32).astype(BF16)
        for m in range(cols // LANES):
            out_ref[p, :, m * LANES : (m + 1) * LANES] = result[m * rows : (m + 1) * rows]
        return carry

    lax.fori_loop(0, owners, patch, 0)


def detect(coadd, before, after, h_rows, h_cols):
    extended = jnp.concatenate([before, coadd, after], axis=0)
    blurred = jnp.dot(h_rows, extended, preferred_element_type=F32, precision=lax.Precision.HIGHEST).astype(BF16)
    rows, cols = blurred.shape
    edge = jnp.zeros((rows, LANES), BF16)
    padded = jnp.concatenate([edge, blurred, edge], axis=1)
    windows = jnp.concatenate([padded[:, m * LANES : (m + 3) * LANES] for m in range(cols // LANES)], axis=0)
    result = jnp.dot(windows, h_cols, preferred_element_type=F32)
    return jnp.concatenate([result[m * rows : (m + 1) * rows] for m in range(cols // LANES)], axis=1)


def reduce_kernel(
    owners,
    part, w_part, h_rows, h_cols, coadd_ref, detection_ref,
    pair_in, sums, arrived, w_pair, w_sums, w_arrived, halos,
    pair_send, pair_recv, w_pair_sems, send, recv, w_send, w_recv, last_sems, halo_send, halo_recv,
):
    me, core = lax.axis_index("patch"), lax.axis_index("visit")
    other = 1 - core
    rows = part.shape[1]
    half = rows // 2
    mine, theirs = pl.ds(core * half, half), pl.ds(other * half, half)

    barrier = pltpu.get_barrier_semaphore()

    def greet(i, carry):
        flat = (me * 2 + core + i) % (2 * owners)
        pl.semaphore_signal(barrier, inc=1, device_id={"patch": flat // 2, "visit": flat % 2}, device_id_type=MESH)
        return carry

    lax.fori_loop(1, 2 * owners, greet, 0)
    pl.semaphore_wait(barrier, 2 * owners - 1)

    def pair_copy(q):
        return pltpu.make_async_remote_copy(
            part.at[q, theirs], pair_in.at[q], pair_send.at[q], pair_recv.at[q],
            device_id={"visit": other}, device_id_type=MESH,
        )

    w_copy = pltpu.make_async_remote_copy(
        w_part, w_pair, w_pair_sems.at[0], w_pair_sems.at[1], device_id={"visit": other}, device_id_type=MESH
    )

    def out_copy(q, slot):
        return pltpu.make_async_remote_copy(
            sums.at[q], arrived.at[slot], send.at[q], recv.at[slot], device_id={"patch": q}, device_id_type=MESH
        )

    def w_out_copy(q, slot):
        return pltpu.make_async_remote_copy(
            w_sums.at[q], w_arrived.at[slot], w_send.at[q], w_recv.at[slot], device_id={"patch": q}, device_id_type=MESH
        )

    w_copy.start()

    def start_pair(i, carry):
        pair_copy((me + i) % owners).start()
        return carry

    lax.fori_loop(1, owners + 1, start_pair, 0)
    w_copy.wait()
    w_sums[...] = w_part[...] + w_pair[...]

    def forward(i, carry):
        q = (me + i) % owners
        pair_copy(q).wait()
        sums[q] = (part[q, mine].astype(F32) + pair_in[q].astype(F32)).astype(BF16)
        out_copy(q, me).start()
        w_out_copy(q, me).start()
        return carry

    lax.fori_loop(1, owners, forward, 0)
    pair_copy(me).wait()
    total = part[me, mine].astype(F32) + pair_in[me].astype(F32)

    def collect(i, carry):
        total, weight = carry
        q = (me + owners - i) % owners
        out_copy(q, q).wait_recv()
        w_out_copy(q, q).wait_recv()
        return total + arrived[q].astype(F32), weight + w_arrived[q]

    total, weight = lax.fori_loop(1, owners, collect, (total, w_sums[me]))
    coadd_ref[mine] = total / jnp.sqrt(weight[0:1, 0:1])

    last = pltpu.make_async_remote_copy(
        coadd_ref.at[mine], coadd_ref.at[mine], last_sems.at[0], last_sems.at[1],
        device_id={"visit": other}, device_id_type=MESH,
    )
    last.start()
    neighbour = (me + owners - 1 + 2 * core) % owners
    border = pl.ds(core * (rows - HALO), HALO)

    def halo_copy(to):
        return pltpu.make_async_remote_copy(
            coadd_ref.at[border], halos.at[other], halo_send.at[to], halo_recv.at[other],
            device_id={"patch": neighbour, "visit": to}, device_id_type=MESH,
        )

    for to in range(2):
        halo_copy(to).start()

    def finish(i, carry):
        q = (me + i) % owners
        out_copy(q, me).wait_send()
        w_out_copy(q, me).wait_send()
        return carry

    lax.fori_loop(1, owners, finish, 0)
    for to in range(2):
        halo_copy(to).wait_send()
    for side in range(2):
        pltpu.make_async_remote_copy(
            coadd_ref.at[border], halos.at[side], halo_send.at[0], halo_recv.at[side],
            device_id={"patch": neighbour, "visit": other}, device_id_type=MESH,
        ).wait_recv()
    last.wait()
    before = jnp.where(me > 0, halos[0], 0.0)
    after = jnp.where(me < owners - 1, halos[1], 0.0)
    detection_ref[...] = detect(coadd_ref[...], before, after, h_rows[...], h_cols[...])


def slot_tables(tile_patch, offsets, psf_coefs, weights, owners, capacity, rows):
    count = tile_patch.shape[0]
    positions = jnp.arange(count, dtype=jnp.int32)
    earlier = positions[:, None] > positions[None, :]
    rank = jnp.sum(earlier & (tile_patch[:, None] == tile_patch[None, :]), axis=1).astype(jnp.int32)
    slot_of = tile_patch * capacity + rank
    slots = jnp.arange(owners * capacity, dtype=jnp.int32)
    source = jnp.sum(jnp.where(slot_of[None, :] == slots[:, None], positions[None, :], 0), axis=1)
    shift = offsets.astype(F32) / 64.0
    distance = jnp.arange(-MID, MID + 1, dtype=F32)
    taps = lanczos(distance[None, :, None] + shift[:, None, :]).astype(BF16)
    weight = weights.astype(F32)
    factor = weight[:, None] * (psf_coefs.astype(F32) / 64.0)
    high, low = split_high_low(factor)
    spare = jnp.zeros((count, 32 - TAPS - 6), BF16)
    meta = jnp.concatenate([taps[:, :, 0], high, low, spare], axis=1)
    lanes = jnp.arange(owners * capacity * rows, dtype=jnp.int32) // rows
    spread = (slot_of[:, None] == lanes[None, :]).astype(BF16)
    meta = lax.dot_general(meta, spread, (((0,), (0,)), ((), ())), preferred_element_type=F32)
    col_taps = taps[:, :, 1].astype(F32).reshape(-1)
    named = tile_patch[None, :] == jnp.arange(owners, dtype=jnp.int32)[:, None]
    weight_sq = jnp.sum(jnp.where(named, (weight * weight)[None, :], 0.0), axis=1)
    return source, col_taps, meta, jnp.broadcast_to(weight_sq[:, None, None], (owners, 8, LANES))


def shards(visit_tiles, tile_patch, offsets, psf_coefs, weights):
    count, rows, cols = visit_tiles.shape
    owners = lax.axis_size("patch")
    capacity = max(2, 2 * count // owners)
    capacity += capacity % 2
    chunk = math.gcd(count, 8)
    wide = cols + LANES
    half = rows // 2

    index = np.arange(rows)
    g_rows = np.concatenate([gaussian(index[:, None] - index[None, :], s, PSF_REACH) for s in PSF_SIGMAS])
    g_high, g_low = split_high_low(g_rows)
    window = np.arange(2 * LANES)
    lane = np.arange(LANES)
    g_cols = np.concatenate([gaussian(HALF + lane[None, :] - window[:, None], s, PSF_REACH) for s in PSF_SIGMAS])
    g_cols = jnp.asarray(g_cols).astype(BF16)
    extended = np.arange(rows + 2 * HALO)
    h_rows = jnp.asarray(gaussian(HALO + index[:, None] - extended[None, :], HALO / 4.0, HALO))
    h_cols = gaussian(LANES + lane[None, :] - np.arange(3 * LANES)[:, None], HALO / 4.0, HALO)
    h_cols = jnp.asarray(h_cols).astype(BF16)

    source, col_taps, meta, w_part = slot_tables(tile_patch, offsets, psf_coefs, weights, owners, capacity, rows)
    vmem = pl.BlockSpec(memory_space=pltpu.VMEM)
    smem = pl.BlockSpec(memory_space=pltpu.SMEM)
    part = pl.pallas_call(
        functools.partial(stack_kernel, owners, capacity, chunk),
        out_shape=jax.ShapeDtypeStruct((owners, rows, cols), BF16),
        in_specs=[smem, smem, pl.BlockSpec(memory_space=pl.ANY), vmem, vmem, vmem, vmem],
        out_specs=vmem,
        scratch_shapes=[
            pltpu.VMEM((count, rows, cols), BF16),
            pltpu.VMEM((count, rows, wide), BF16),
            pltpu.VMEM((3 * rows, wide), BF16),
            pltpu.SemaphoreType.DMA((count // chunk,)),
        ],
        compiler_params=pltpu.CompilerParams(vmem_limit_bytes=48 * 2**20),
        name="stack",
    )(source, col_taps, visit_tiles, meta, g_high, g_low, g_cols)

    dma = pltpu.SemaphoreType.DMA
    return pl.pallas_call(
        functools.partial(reduce_kernel, owners),
        out_shape=(jax.ShapeDtypeStruct((rows, cols), F32), jax.ShapeDtypeStruct((rows, cols), F32)),
        in_specs=[vmem, vmem, vmem, vmem],
        out_specs=(vmem, vmem),
        scratch_shapes=[
            pltpu.VMEM((owners, half, cols), BF16),
            pltpu.VMEM((owners, half, cols), BF16),
            pltpu.VMEM((owners, half, cols), BF16),
            pltpu.VMEM((owners, 8, LANES), F32),
            pltpu.VMEM((owners, 8, LANES), F32),
            pltpu.VMEM((owners, 8, LANES), F32),
            pltpu.VMEM((2, HALO, cols), F32),
            dma((owners,)), dma((owners,)), dma((2,)),
            dma((owners,)), dma((owners,)), dma((owners,)), dma((owners,)),
            dma((2,)), dma((2,)), dma((2,)),
        ],
        compiler_params=pltpu.CompilerParams(
            collective_id=0, has_side_effects=True, vmem_limit_bytes=48 * 2**20
        ),
        name="reduce",
    )(part, w_part, h_rows, h_cols)


def solution(mesh):
    placed = (
        P(("groups", "patch", "visit"), None, None),
        P(("groups", "patch", "visit")),
        P(("groups", "patch", "visit"), None),
        P(("groups", "patch", "visit"), None),
        P(("groups", "patch", "visit")),
    )
    return jax.shard_map(
        shards,
        mesh=mesh,
        in_specs=placed,
        out_specs=(P(("groups", "patch"), None), P(("groups", "patch"), None)),
        check_vma=False,
    )
```

```python
import functools
import math

import jax
import jax.numpy as jnp
import numpy as np
from jax import lax
from jax.experimental import pallas as pl
from jax.experimental.pallas import tpu as pltpu
from jax.sharding import PartitionSpec as P

HALO = 8
PSF_SIGMAS = (0.75, 1.5, 3.0)
PSF_REACH = 16
MID = 5
LANES = 128
HALF = 64
MESH = pl.DeviceIdType.MESH
BF16 = jnp.bfloat16
F32 = jnp.float32


def gaussian_taps(sigma, reach):
    distance = np.arange(-reach, reach + 1, dtype=np.float64)
    return np.exp(-distance * distance / (2.0 * sigma * sigma)) / (math.pi * sigma * sigma) ** 0.25


def well_rounded_scale(sigma, reach):
    taps = gaussian_taps(sigma, reach)
    scales = 1.0 + np.arange(1024) / 1024.0
    scaled = taps[None, :] * scales[:, None]
    rounded = scaled.astype(np.float32).astype(BF16).astype(np.float64)
    error = np.sum((rounded - scaled) ** 2, axis=1) / scales**2
    gain = (np.sum(rounded - scaled, axis=1) / scales) ** 2
    return float(scales[np.argmin(error + gain)])


def gaussian(distance, sigma, reach, scale):
    distance = distance.astype(F32)
    shape = jnp.exp(distance * distance * (-0.5 / (sigma * sigma))) * (scale / (math.pi * sigma * sigma) ** 0.25)
    return jnp.where(jnp.abs(distance) <= reach, shape, 0.0)


def row_minus_col(shape):
    return lax.broadcasted_iota(jnp.int32, shape, 0) - lax.broadcasted_iota(jnp.int32, shape, 1)


def split_high_low(matrix):
    high = matrix.astype(BF16)
    return high, (matrix - high.astype(F32)).astype(BF16)


def lanczos(value):
    inside = jnp.abs(value) < 3.0
    return jnp.where(inside, jnp.sinc(value) * jnp.sinc(value / 3.0), 0.0)


LOW, HIGH = HALF - 16, HALF + LANES + 16


def column_warp(tile, table_row):
    rows, cols = tile.shape
    shape = (HIGH - LOW, LANES)
    band = pltpu.roll(jnp.broadcast_to(table_row, shape), 0, axis=1, stride=1, stride_axis=0)
    distance = row_minus_col(shape) - (HALF - LOW)
    band = jnp.where(jnp.abs(distance) <= MID, band, 0.0).astype(BF16)
    matrix = jnp.concatenate([jnp.zeros((LOW, LANES), BF16), band, jnp.zeros((2 * LANES - HIGH, LANES), BF16)], axis=0)
    edge = jnp.zeros((rows, LANES), BF16)
    padded = jnp.concatenate([edge, tile, edge], axis=1)
    blocks = cols // LANES + 1
    windows = jnp.concatenate([padded[:, m * LANES : (m + 2) * LANES] for m in range(blocks)], axis=0)
    return jnp.dot(windows, matrix, preferred_element_type=F32).astype(BF16)


def row_matrices(table_rows, factors, g_high, g_low, rows):
    shape = (rows, LANES)
    per = LANES // rows
    lane_slot = lax.broadcasted_iota(jnp.int32, shape, 1) // rows
    shifts = []
    for first in range(0, len(table_rows), per):
        both = jnp.zeros(shape, F32)
        for s in range(per):
            row = jnp.broadcast_to(table_rows[first + s], shape)
            band = pltpu.roll(row, s * rows, axis=1, stride=1, stride_axis=0)
            both = jnp.where(lane_slot == s, band, both)
        shifts.append(both.astype(BF16))
    shift = jnp.concatenate(shifts, axis=1)
    blurred = jnp.dot(g_high, shift, preferred_element_type=F32) + jnp.dot(g_low, shift, preferred_element_type=F32)
    pieces = []
    for k in range(3):
        factor = factors[k : k + 1, :] + factors[3 + k : 4 + k, :]
        pieces.append(blurred[k * rows : (k + 1) * rows] * factor)
    return jnp.concatenate(pieces, axis=0).astype(BF16)


def detect(coadd, before, after):
    rows, cols = coadd.shape
    sigma = HALO / 4.0
    scale = well_rounded_scale(sigma, HALO)
    extended = jnp.concatenate([before, coadd, after], axis=0)
    h_rows = gaussian(row_minus_col((rows, rows + 2 * HALO)) + HALO, sigma, HALO, 1.0 / scale)
    blurred = jnp.dot(h_rows, extended, preferred_element_type=F32, precision=lax.Precision.HIGHEST).astype(BF16)
    h_cols = gaussian(row_minus_col((3 * LANES, LANES)) - LANES, sigma, HALO, scale).astype(BF16)
    edge = jnp.zeros((rows, LANES), BF16)
    padded = jnp.concatenate([edge, blurred, edge], axis=1)
    windows = jnp.concatenate([padded[:, m * LANES : (m + 3) * LANES] for m in range(cols // LANES)], axis=0)
    result = jnp.dot(windows, h_cols, preferred_element_type=F32)
    return jnp.concatenate([result[m * rows : (m + 1) * rows] for m in range(cols // LANES)], axis=1)


def fused_kernel(
    owners, capacity, chunk,
    source, tiles_hbm, col_table, row_table, factor_ref, w_part,
    coadd_ref, detection_ref,
    tiles, warped, blur, part, g_high, g_low, g_cols, load_sems,
    pair_in, sums, arrived, w_pair, w_sums, w_arrived, halos,
    pair_send, pair_recv, w_pair_sems, send, recv, w_send, w_recv, last_sems, halo_send, halo_recv,
):
    me, core = lax.axis_index("patch"), lax.axis_index("visit")
    other = 1 - core
    count, rows, cols = tiles.shape
    wide = cols + LANES
    half = rows // 2
    chunks = count // chunk
    mine, theirs = pl.ds(core * half, half), pl.ds(other * half, half)

    def load(c):
        span = pl.ds(c * chunk, chunk)
        return pltpu.make_async_copy(tiles_hbm.at[span], tiles.at[span], load_sems.at[c])

    for c in range(chunks):
        load(c).start()

    barrier = pltpu.get_barrier_semaphore()

    def greet(i, carry):
        flat = (me * 2 + core + i) % (2 * owners)
        pl.semaphore_signal(barrier, inc=1, device_id={"patch": flat // 2, "visit": flat % 2}, device_id_type=MESH)
        return carry

    lax.fori_loop(1, 2 * owners, greet, 0)

    for k, sigma in enumerate(PSF_SIGMAS):
        scale = well_rounded_scale(sigma, PSF_REACH)
        high, low = split_high_low(gaussian(row_minus_col((rows, rows)), sigma, PSF_REACH, 1.0 / scale))
        g_high[k * rows : (k + 1) * rows] = high
        g_low[k * rows : (k + 1) * rows] = low
        taps = gaussian(row_minus_col((2 * LANES, LANES)) - HALF, sigma, PSF_REACH, scale)
        g_cols[2 * k * LANES : 2 * (k + 1) * LANES] = taps.astype(BF16)

    def warp_chunk(c, carry):
        load(c).wait()

        def warp(step, carry):
            v = c * chunk + step
            result = column_warp(tiles[v], col_table[pl.ds(v, 1), :])
            for m in range(wide // LANES):
                warped[v, :, m * LANES : (m + 1) * LANES] = result[m * rows : (m + 1) * rows]
            return carry

        return lax.fori_loop(0, chunk, warp, carry, unroll=4 if chunk % 4 == 0 else 1)

    lax.fori_loop(0, chunks, warp_chunk, 0)

    pl.semaphore_wait(barrier, 2 * owners - 1)

    def pair_copy(q):
        return pltpu.make_async_remote_copy(
            part.at[q, theirs], pair_in.at[q], pair_send.at[q], pair_recv.at[q],
            device_id={"visit": other}, device_id_type=MESH,
        )

    w_copy = pltpu.make_async_remote_copy(
        w_part, w_pair, w_pair_sems.at[0], w_pair_sems.at[1], device_id={"visit": other}, device_id_type=MESH
    )

    def out_copy(q, slot):
        return pltpu.make_async_remote_copy(
            sums.at[q], arrived.at[slot], send.at[q], recv.at[slot], device_id={"patch": q}, device_id_type=MESH
        )

    def w_out_copy(q, slot):
        return pltpu.make_async_remote_copy(
            w_sums.at[q], w_arrived.at[slot], w_send.at[q], w_recv.at[slot], device_id={"patch": q}, device_id_type=MESH
        )

    w_copy.start()

    depth = capacity * rows
    pieces = [(a, min(a + 3 * LANES, wide)) for a in range(0, wide, 3 * LANES)]

    def compute(p):
        factors = factor_ref[:, pl.ds(pl.multiple_of(p * depth, LANES), depth)]
        table_rows = [row_table[pl.ds(p * capacity + r, 1), :] for r in range(capacity)]
        left = row_matrices(table_rows, factors, g_high[...], g_low[...], rows)
        slots = [source[p * capacity + r] for r in range(capacity)]
        for a, b in pieces:
            right = jnp.concatenate([warped[s, :, a:b] for s in slots], axis=0)
            total = jnp.dot(left, right, preferred_element_type=F32)
            lane = a + lax.broadcasted_iota(jnp.int32, total.shape, 1)
            if a < HALF or b > wide - HALF:
                total = jnp.where((lane >= HALF) & (lane < wide - HALF), total, 0.0)
            blur[:, a:b] = total.astype(BF16)
        windows = jnp.concatenate(
            [
                jnp.concatenate([blur[k * rows : (k + 1) * rows, m * LANES : (m + 2) * LANES] for k in range(3)], axis=1)
                for m in range(cols // LANES)
            ],
            axis=0,
        )
        result = jnp.dot(windows, g_cols[...], preferred_element_type=F32).astype(BF16)
        for m in range(cols // LANES):
            part[p, :, m * LANES : (m + 1) * LANES] = result[m * rows : (m + 1) * rows]
        pair_copy(p).start()

    def forward(q):
        pair_copy(q).wait()
        sums[q] = (part[q, mine].astype(F32) + pair_in[q].astype(F32)).astype(BF16)
        out_copy(q, me).start()
        w_out_copy(q, me).start()

    compute((me + 1) % owners)
    w_copy.wait()
    w_sums[...] = w_part[...] + w_pair[...]

    def patch(i, carry):
        compute((me + i) % owners)
        forward((me + i - 1) % owners)
        return carry

    lax.fori_loop(2, owners + 1, patch, 0)
    pair_copy(me).wait()
    total = part[me, mine].astype(F32) + pair_in[me].astype(F32)

    def collect(i, carry):
        total, weight = carry
        q = (me + owners - i) % owners
        out_copy(q, q).wait_recv()
        w_out_copy(q, q).wait_recv()
        return total + arrived[q].astype(F32), weight + w_arrived[q]

    total, weight = lax.fori_loop(1, owners, collect, (total, w_sums[me]))
    coadd_ref[mine] = total / jnp.sqrt(weight[0:1, 0:1])

    last = pltpu.make_async_remote_copy(
        coadd_ref.at[mine], coadd_ref.at[mine], last_sems.at[0], last_sems.at[1],
        device_id={"visit": other}, device_id_type=MESH,
    )
    last.start()
    neighbour = (me + owners - 1 + 2 * core) % owners
    border = pl.ds(core * (rows - HALO), HALO)

    def halo_copy(to):
        return pltpu.make_async_remote_copy(
            coadd_ref.at[border], halos.at[other], halo_send.at[to], halo_recv.at[other],
            device_id={"patch": neighbour, "visit": to}, device_id_type=MESH,
        )

    for to in range(2):
        halo_copy(to).start()

    def finish(i, carry):
        q = (me + i) % owners
        out_copy(q, me).wait_send()
        w_out_copy(q, me).wait_send()
        return carry

    lax.fori_loop(1, owners, finish, 0)
    for to in range(2):
        halo_copy(to).wait_send()
    for side in range(2):
        pltpu.make_async_remote_copy(
            coadd_ref.at[border], halos.at[side], halo_send.at[0], halo_recv.at[side],
            device_id={"patch": neighbour, "visit": other}, device_id_type=MESH,
        ).wait_recv()
    last.wait()
    before = jnp.where(me > 0, halos[0], 0.0)
    after = jnp.where(me < owners - 1, halos[1], 0.0)
    detection_ref[...] = detect(coadd_ref[...], before, after)


def slot_tables(tile_patch, offsets, psf_coefs, weights, owners, capacity, rows):
    count = tile_patch.shape[0]
    positions = jnp.arange(count, dtype=jnp.int32)
    earlier = positions[:, None] > positions[None, :]
    rank = jnp.sum(earlier & (tile_patch[:, None] == tile_patch[None, :]), axis=1).astype(jnp.int32)
    slot_of = tile_patch * capacity + rank
    slots = jnp.arange(owners * capacity, dtype=jnp.int32)
    chosen = slot_of[None, :] == slots[:, None]
    source = jnp.sum(jnp.where(chosen, positions[None, :], 0), axis=1)
    shift = offsets.astype(F32) / 64.0
    lane = jnp.arange(LANES, dtype=jnp.int32)[None, :]
    col_table = lanczos((lane - LANES + HALF - LOW).astype(F32) + shift[:, 1:2]).astype(BF16).astype(F32)
    row_table = lanczos(jnp.where(lane < HALF, -lane, LANES - lane).astype(F32) + shift[:, 0:1]).astype(BF16)
    row_table = jnp.dot(chosen.astype(BF16), row_table, preferred_element_type=F32)
    weight = weights.astype(F32)
    factor = weight[:, None] * (psf_coefs.astype(F32) / 64.0)
    high, low = split_high_low(factor)
    both = jnp.concatenate([high, low, jnp.zeros((count, 2), BF16)], axis=1)
    lanes = jnp.arange(owners * capacity * rows, dtype=jnp.int32) // rows
    spread = (slot_of[:, None] == lanes[None, :]).astype(BF16)
    factors = lax.dot_general(both, spread, (((0,), (0,)), ((), ())), preferred_element_type=F32)
    named = tile_patch[None, :] == jnp.arange(owners, dtype=jnp.int32)[:, None]
    weight_sq = jnp.sum(jnp.where(named, (weight * weight)[None, :], 0.0), axis=1)
    return source, col_table, row_table, factors, jnp.broadcast_to(weight_sq[:, None, None], (owners, 8, LANES))


def shards(visit_tiles, tile_patch, offsets, psf_coefs, weights):
    count, rows, cols = visit_tiles.shape
    owners = lax.axis_size("patch")
    capacity = max(2, 2 * count // owners)
    capacity += capacity % 2
    chunk = math.gcd(count, 8)
    wide = cols + LANES
    half = rows // 2
    tables = slot_tables(tile_patch, offsets, psf_coefs, weights, owners, capacity, rows)
    source, col_table, row_table, factors, w_part = tables
    vmem = pl.BlockSpec(memory_space=pltpu.VMEM)
    smem = pl.BlockSpec(memory_space=pltpu.SMEM)
    dma = pltpu.SemaphoreType.DMA
    return pl.pallas_call(
        functools.partial(fused_kernel, owners, capacity, chunk),
        out_shape=(jax.ShapeDtypeStruct((rows, cols), F32), jax.ShapeDtypeStruct((rows, cols), F32)),
        in_specs=[smem, pl.BlockSpec(memory_space=pl.ANY), vmem, vmem, vmem, vmem],
        out_specs=(vmem, vmem),
        scratch_shapes=[
            pltpu.VMEM((count, rows, cols), BF16),
            pltpu.VMEM((count, rows, wide), BF16),
            pltpu.VMEM((3 * rows, wide), BF16),
            pltpu.VMEM((owners, rows, cols), BF16),
            pltpu.VMEM((3 * rows, rows), BF16),
            pltpu.VMEM((3 * rows, rows), BF16),
            pltpu.VMEM((6 * LANES, LANES), BF16),
            dma((count // chunk,)),
            pltpu.VMEM((owners, half, cols), BF16),
            pltpu.VMEM((owners, half, cols), BF16),
            pltpu.VMEM((owners, half, cols), BF16),
            pltpu.VMEM((owners, 8, LANES), F32),
            pltpu.VMEM((owners, 8, LANES), F32),
            pltpu.VMEM((owners, 8, LANES), F32),
            pltpu.VMEM((2, HALO, cols), F32),
            dma((owners,)), dma((owners,)), dma((2,)),
            dma((owners,)), dma((owners,)), dma((owners,)), dma((owners,)),
            dma((2,)), dma((2,)), dma((2,)),
        ],
        compiler_params=pltpu.CompilerParams(
            collective_id=0, has_side_effects=True, vmem_limit_bytes=52 * 2**20
        ),
        name="fused",
    )(source, visit_tiles, col_table, row_table, factors, w_part)


def solution(mesh):
    placed = (
        P(("groups", "patch", "visit"), None, None),
        P(("groups", "patch", "visit")),
        P(("groups", "patch", "visit"), None),
        P(("groups", "patch", "visit"), None),
        P(("groups", "patch", "visit")),
    )
    return jax.shard_map(
        shards,
        mesh=mesh,
        in_specs=placed,
        out_specs=(P(("groups", "patch"), None), P(("groups", "patch"), None)),
        check_vma=False,
    )
```

```python
import functools
import math

import jax
import jax.numpy as jnp
import numpy as np
from jax import lax
from jax.experimental import pallas as pl
from jax.experimental.pallas import tpu as pltpu
from jax.sharding import PartitionSpec as P

HALO = 8
PSF_SIGMAS = (0.75, 1.5, 3.0)
PSF_REACH = 16
MID = 5
LANES = 128
HALF = 64
MESH = pl.DeviceIdType.MESH
BF16 = jnp.bfloat16
F32 = jnp.float32


def gaussian_taps(sigma, reach):
    distance = np.arange(-reach, reach + 1, dtype=np.float64)
    return np.exp(-distance * distance / (2.0 * sigma * sigma)) / (math.pi * sigma * sigma) ** 0.25


def well_rounded_scale(sigma, reach):
    taps = gaussian_taps(sigma, reach)
    scales = 1.0 + np.arange(1024) / 1024.0
    scaled = taps[None, :] * scales[:, None]
    rounded = scaled.astype(np.float32).astype(BF16).astype(np.float64)
    error = np.sum((rounded - scaled) ** 2, axis=1) / scales**2
    gain = (np.sum(rounded - scaled, axis=1) / scales) ** 2
    return float(scales[np.argmin(error + gain)])


def gaussian(distance, sigma, reach, scale):
    distance = distance.astype(F32)
    shape = jnp.exp(distance * distance * (-0.5 / (sigma * sigma))) * (scale / (math.pi * sigma * sigma) ** 0.25)
    return jnp.where(jnp.abs(distance) <= reach, shape, 0.0)


def row_minus_col(shape):
    return lax.broadcasted_iota(jnp.int32, shape, 0) - lax.broadcasted_iota(jnp.int32, shape, 1)


def split_high_low(matrix):
    high = matrix.astype(BF16)
    return high, (matrix - high.astype(F32)).astype(BF16)


def sinc(value):
    angle = jnp.where(value == 0.0, 1.0, math.pi * value)
    return jnp.where(value == 0.0, 1.0, jnp.sin(angle) / angle)


def lanczos(value):
    inside = jnp.abs(value) < 3.0
    value = jnp.where(inside, value, 0.0)
    return jnp.where(inside, sinc(value) * sinc(value / 3.0), 0.0)


LOW, HIGH = HALF - 16, HALF + LANES + 16


def column_warp(tile, table_row):
    rows, cols = tile.shape
    shape = (HIGH - LOW, LANES)
    band = pltpu.roll(jnp.broadcast_to(table_row, shape), 0, axis=1, stride=1, stride_axis=0)
    distance = row_minus_col(shape) - (HALF - LOW)
    band = jnp.where(jnp.abs(distance) <= MID, band, 0.0).astype(BF16)
    matrix = jnp.concatenate([jnp.zeros((LOW, LANES), BF16), band, jnp.zeros((2 * LANES - HIGH, LANES), BF16)], axis=0)
    edge = jnp.zeros((rows, LANES), BF16)
    padded = jnp.concatenate([edge, tile, edge], axis=1)
    blocks = cols // LANES + 1
    windows = jnp.concatenate([padded[:, m * LANES : (m + 2) * LANES] for m in range(blocks)], axis=0)
    return jnp.dot(windows, matrix, preferred_element_type=F32).astype(BF16)


def row_matrices(table_rows, factors, g_rows, rows):
    shape = (rows, LANES)
    per = LANES // rows
    lane_slot = lax.broadcasted_iota(jnp.int32, shape, 1) // rows
    shifts = []
    for first in range(0, len(table_rows), per):
        both = jnp.zeros(shape, F32)
        for s in range(per):
            row = jnp.broadcast_to(table_rows[first + s], shape)
            band = pltpu.roll(row, s * rows, axis=1, stride=1, stride_axis=0)
            both = jnp.where(lane_slot == s, band, both)
        shifts.append(both.astype(BF16))
    shift = jnp.concatenate(shifts, axis=1)
    blurred = jnp.dot(g_rows, jnp.concatenate([shift, shift], axis=0), preferred_element_type=F32)
    pieces = []
    for k in range(3):
        factor = factors[k : k + 1, :] + factors[3 + k : 4 + k, :]
        pieces.append(blurred[k * rows : (k + 1) * rows] * factor)
    return jnp.concatenate(pieces, axis=0).astype(BF16)


def detect(coadd, before, after):
    rows, cols = coadd.shape
    sigma = HALO / 4.0
    scale = well_rounded_scale(sigma, HALO)
    extended = jnp.concatenate([before, coadd, after], axis=0)
    h_rows = gaussian(row_minus_col((rows, rows + 2 * HALO)) + HALO, sigma, HALO, 1.0 / scale)
    blurred = jnp.dot(h_rows, extended, preferred_element_type=F32, precision=lax.Precision.HIGHEST).astype(BF16)
    h_cols = gaussian(row_minus_col((3 * LANES, LANES)) - LANES, sigma, HALO, scale).astype(BF16)
    edge = jnp.zeros((rows, LANES), BF16)
    padded = jnp.concatenate([edge, blurred, edge], axis=1)
    windows = jnp.concatenate([padded[:, m * LANES : (m + 3) * LANES] for m in range(cols // LANES)], axis=0)
    result = jnp.dot(windows, h_cols, preferred_element_type=F32)
    return jnp.concatenate([result[m * rows : (m + 1) * rows] for m in range(cols // LANES)], axis=1)


def slot_tables(named, offsets, coefs, weights, owners, capacity):
    count = named.shape[1]
    slots = owners * capacity
    square = (count, count)
    sublane, lane = lax.broadcasted_iota(jnp.int32, square, 0), lax.broadcasted_iota(jnp.int32, square, 1)

    def to_column(row):
        spread = jnp.where(sublane == lane, jnp.broadcast_to(row, square), jnp.zeros(square, row.dtype))
        return jnp.sum(spread, axis=1, keepdims=True)

    named_column = to_column(named)
    same = jnp.where(jnp.broadcast_to(named, square) == jnp.broadcast_to(named_column, square), 1, 0)
    rank_row = jnp.sum(jnp.where(sublane < lane, same, 0), axis=0, keepdims=True)
    rank_column = jnp.sum(jnp.where(lane < sublane, same, 0), axis=1, keepdims=True)
    slot_row = named * capacity + rank_row
    slot_column = named_column * capacity + rank_column

    chosen = lax.broadcasted_iota(jnp.int32, (slots, count), 0) == slot_row
    place = lax.broadcasted_iota(jnp.int32, (count, slots), 1) == slot_column
    tile = lax.broadcasted_iota(jnp.int32, (count, slots), 0)
    source = jnp.sum(jnp.where(place, tile, 0), axis=0, keepdims=True)

    shift = offsets.astype(F32) / 64.0
    at = lax.broadcasted_iota(jnp.int32, (count, LANES), 1)
    col_table = lanczos((at - LANES + HALF - LOW).astype(F32) + to_column(shift[1:2]))
    col_table = col_table.astype(BF16).astype(F32)
    row_table = lanczos(jnp.where(at < HALF, -at, LANES - at).astype(F32) + to_column(shift[0:1]))
    one = jnp.where(chosen, 1.0, 0.0).astype(BF16)
    row_table = jnp.dot(one, row_table.astype(BF16), preferred_element_type=F32)
    factor = weights * (coefs.astype(F32) / 64.0)
    high, low = split_high_low(factor)
    rest = jnp.zeros((2, count), F32)
    factors = jnp.concatenate([high.astype(F32), low.astype(F32), rest], axis=0).astype(BF16)
    return col_table, row_table, factors, slot_column, source


def fused_kernel(
    owners, capacity, chunk,
    tiles_hbm, args_ref, weight_ref,
    coadd_ref, detection_ref,
    tiles, warped, blur, part, g_rows, g_cols, load_sems,
    col_table, row_table, factor_rows, slot_column, w_part, source_row, source, source_sem,
    pair_in, sums, arrived, w_pair, w_sums, w_arrived, halos,
    pair_send, pair_recv, w_pair_sems, send, recv, w_send, w_recv, last_sems, halo_send, halo_recv,
):
    me, core = lax.axis_index("patch"), lax.axis_index("visit")
    other = 1 - core
    count, rows, cols = tiles.shape
    wide = cols + LANES
    half = rows // 2
    chunks = count // chunk
    mine, theirs = pl.ds(core * half, half), pl.ds(other * half, half)

    def load(c):
        span = pl.ds(c * chunk, chunk)
        return pltpu.make_async_copy(tiles_hbm.at[span], tiles.at[span], load_sems.at[c])

    for c in range(chunks):
        load(c).start()

    barrier = pltpu.get_barrier_semaphore()

    def greet(i, carry):
        flat = (me * 2 + core + i) % (2 * owners)
        pl.semaphore_signal(barrier, inc=1, device_id={"patch": flat // 2, "visit": flat % 2}, device_id_type=MESH)
        return carry

    lax.fori_loop(1, 2 * owners, greet, 0)

    for k, sigma in enumerate(PSF_SIGMAS):
        scale = well_rounded_scale(sigma, PSF_REACH)
        high, low = split_high_low(gaussian(row_minus_col((rows, rows)), sigma, PSF_REACH, 1.0 / scale))
        g_rows[k * rows : (k + 1) * rows] = jnp.concatenate([high, low], axis=1)
        taps = gaussian(row_minus_col((2 * LANES, LANES)) - HALF, sigma, PSF_REACH, scale)
        g_cols[2 * k * LANES : 2 * (k + 1) * LANES] = taps.astype(BF16)

    args = args_ref[...]
    named, weight = args[0:1], weight_ref[...]
    col_values, row_values, factor_values, column, row = slot_tables(
        named, args[1:3], args[3:6], weight, owners, capacity
    )
    source_row[...] = row
    source_copy = pltpu.make_async_copy(source_row, source, source_sem)
    source_copy.start()
    col_table[...] = col_values
    row_table[...] = row_values
    factor_rows[...] = factor_values
    slot_column[...] = column
    for p in range(owners):
        here = jnp.where(named == p, weight * weight, 0.0)
        w_part[p] = jnp.broadcast_to(jnp.sum(here, axis=1, keepdims=True), (8, LANES))

    def warp_chunk(c, carry):
        load(c).wait()

        def warp(step, carry):
            v = c * chunk + step
            result = column_warp(tiles[v], col_table[pl.ds(v, 1), :])
            for m in range(wide // LANES):
                warped[v, :, m * LANES : (m + 1) * LANES] = result[m * rows : (m + 1) * rows]
            return carry

        return lax.fori_loop(0, chunk, warp, carry, unroll=4 if chunk % 4 == 0 else 1)

    lax.fori_loop(0, chunks, warp_chunk, 0)
    source_copy.wait()

    pl.semaphore_wait(barrier, 2 * owners - 1)

    def pair_copy(q):
        return pltpu.make_async_remote_copy(
            part.at[q, theirs], pair_in.at[q], pair_send.at[q], pair_recv.at[q],
            device_id={"visit": other}, device_id_type=MESH,
        )

    w_copy = pltpu.make_async_remote_copy(
        w_part, w_pair, w_pair_sems.at[0], w_pair_sems.at[1], device_id={"visit": other}, device_id_type=MESH
    )

    def out_copy(q, slot):
        return pltpu.make_async_remote_copy(
            sums.at[q], arrived.at[slot], send.at[q], recv.at[slot], device_id={"patch": q}, device_id_type=MESH
        )

    def w_out_copy(q, slot):
        return pltpu.make_async_remote_copy(
            w_sums.at[q], w_arrived.at[slot], w_send.at[q], w_recv.at[slot], device_id={"patch": q}, device_id_type=MESH
        )

    w_copy.start()

    depth = capacity * rows
    pieces = [(a, min(a + 2 * LANES, wide)) for a in range(0, wide, 2 * LANES)]

    def compute(p):
        lane_slot = p * capacity + lax.broadcasted_iota(jnp.int32, (count, depth), 1) // rows
        spread = jnp.where(slot_column[...] == lane_slot, 1.0, 0.0).astype(BF16)
        factors = jnp.dot(factor_rows[...], spread, preferred_element_type=F32)
        table_rows = [row_table[pl.ds(p * capacity + r, 1), :] for r in range(capacity)]
        left = row_matrices(table_rows, factors, g_rows[...], rows)
        slots = [jnp.clip(source[0, p * capacity + r], 0, count - 1) for r in range(capacity)]
        for a, b in pieces:
            right = jnp.concatenate([warped[s, :, a:b] for s in slots], axis=0)
            total = jnp.dot(left, right, preferred_element_type=F32)
            lane = a + lax.broadcasted_iota(jnp.int32, total.shape, 1)
            if a < HALF or b > wide - HALF:
                total = jnp.where((lane >= HALF) & (lane < wide - HALF), total, 0.0)
            blur[:, a:b] = total.astype(BF16)
        windows = jnp.concatenate(
            [
                jnp.concatenate([blur[k * rows : (k + 1) * rows, m * LANES : (m + 2) * LANES] for k in range(3)], axis=1)
                for m in range(cols // LANES)
            ],
            axis=0,
        )
        result = jnp.dot(windows, g_cols[...], preferred_element_type=F32).astype(BF16)
        for m in range(cols // LANES):
            part[p, :, m * LANES : (m + 1) * LANES] = result[m * rows : (m + 1) * rows]
        pair_copy(p).start()

    def forward(q):
        pair_copy(q).wait()
        sums[q] = (part[q, mine].astype(F32) + pair_in[q].astype(F32)).astype(BF16)
        out_copy(q, me).start()
        w_out_copy(q, me).start()

    compute((me + 1) % owners)
    w_copy.wait()
    w_sums[...] = w_part[...] + w_pair[...]

    def patch(i, carry):
        compute((me + i) % owners)
        forward((me + i - 1) % owners)
        return carry

    lax.fori_loop(2, owners + 1, patch, 0)
    pair_copy(me).wait()
    total = part[me, mine].astype(F32) + pair_in[me].astype(F32)

    def collect(i, carry):
        total, weight = carry
        q = (me + owners - i) % owners
        out_copy(q, q).wait_recv()
        w_out_copy(q, q).wait_recv()
        return total + arrived[q].astype(F32), weight + w_arrived[q]

    total, weight = lax.fori_loop(1, owners, collect, (total, w_sums[me]))
    coadd_ref[mine] = total / jnp.sqrt(weight[0:1, 0:1])

    last = pltpu.make_async_remote_copy(
        coadd_ref.at[mine], coadd_ref.at[mine], last_sems.at[0], last_sems.at[1],
        device_id={"visit": other}, device_id_type=MESH,
    )
    last.start()
    neighbour = (me + owners - 1 + 2 * core) % owners
    border = pl.ds(core * (rows - HALO), HALO)

    def halo_copy(to):
        return pltpu.make_async_remote_copy(
            coadd_ref.at[border], halos.at[other], halo_send.at[to], halo_recv.at[other],
            device_id={"patch": neighbour, "visit": to}, device_id_type=MESH,
        )

    for to in range(2):
        halo_copy(to).start()

    def finish(i, carry):
        q = (me + i) % owners
        out_copy(q, me).wait_send()
        w_out_copy(q, me).wait_send()
        return carry

    lax.fori_loop(1, owners, finish, 0)
    for to in range(2):
        halo_copy(to).wait_send()
    for side in range(2):
        pltpu.make_async_remote_copy(
            coadd_ref.at[border], halos.at[side], halo_send.at[0], halo_recv.at[side],
            device_id={"patch": neighbour, "visit": other}, device_id_type=MESH,
        ).wait_recv()
    last.wait()
    before = jnp.where(me > 0, halos[0], 0.0)
    after = jnp.where(me < owners - 1, halos[1], 0.0)
    detection_ref[...] = detect(coadd_ref[...], before, after)


def shards(visit_tiles, tile_patch, offsets, psf_coefs, weights):
    count, rows, cols = visit_tiles.shape
    owners = lax.axis_size("patch")
    capacity = max(2, 2 * count // owners)
    capacity += capacity % 2
    chunk = math.gcd(count, 8)
    wide = cols + LANES
    half = rows // 2
    args, first = jnp.zeros((8, count), jnp.int32), 0
    for array in (tile_patch[None, :], offsets.T, psf_coefs.T):
        last = first + array.shape[0]
        args = args + jnp.pad(array, ((first, 8 - last), (0, 0)))
        first = last
    vmem = pl.BlockSpec(memory_space=pltpu.VMEM)
    hbm = pl.BlockSpec(memory_space=pltpu.HBM)
    dma = pltpu.SemaphoreType.DMA
    return pl.pallas_call(
        functools.partial(fused_kernel, owners, capacity, chunk),
        out_shape=(jax.ShapeDtypeStruct((rows, cols), F32), jax.ShapeDtypeStruct((rows, cols), F32)),
        in_specs=[hbm, vmem, vmem],
        out_specs=(vmem, vmem),
        scratch_shapes=[
            pltpu.VMEM((count, rows, cols), BF16),
            pltpu.VMEM((count, rows, wide), BF16),
            pltpu.VMEM((3 * rows, wide), BF16),
            pltpu.VMEM((owners, rows, cols), BF16),
            pltpu.VMEM((3 * rows, 2 * rows), BF16),
            pltpu.VMEM((6 * LANES, LANES), BF16),
            dma((count // chunk,)),
            pltpu.VMEM((count, LANES), F32),
            pltpu.VMEM((owners * capacity, LANES), F32),
            pltpu.VMEM((8, count), BF16),
            pltpu.VMEM((count, 1), jnp.int32),
            pltpu.VMEM((owners, 8, LANES), F32),
            pltpu.VMEM((1, owners * capacity), jnp.int32),
            pltpu.SMEM((1, owners * capacity), jnp.int32),
            dma(()),
            pltpu.VMEM((owners, half, cols), BF16),
            pltpu.VMEM((owners, half, cols), BF16),
            pltpu.VMEM((owners, half, cols), BF16),
            pltpu.VMEM((owners, 8, LANES), F32),
            pltpu.VMEM((owners, 8, LANES), F32),
            pltpu.VMEM((owners, 8, LANES), F32),
            pltpu.VMEM((2, HALO, cols), F32),
            dma((owners,)), dma((owners,)), dma((2,)),
            dma((owners,)), dma((owners,)), dma((owners,)), dma((owners,)),
            dma((2,)), dma((2,)), dma((2,)),
        ],
        compiler_params=pltpu.CompilerParams(
            collective_id=0, has_side_effects=True, vmem_limit_bytes=52 * 2**20
        ),
        name="fused",
    )(visit_tiles, args, weights.astype(F32)[None, :])


def solution(mesh):
    placed = (
        P(("groups", "patch", "visit"), None, None),
        P(("groups", "patch", "visit")),
        P(("groups", "patch", "visit"), None),
        P(("groups", "patch", "visit"), None),
        P(("groups", "patch", "visit")),
    )
    return jax.shard_map(
        shards,
        mesh=mesh,
        in_specs=placed,
        out_specs=(P(("groups", "patch"), None), P(("groups", "patch"), None)),
        check_vma=False,
    )
```

```python
import functools
import math

import jax
import jax.numpy as jnp
import numpy as np
from jax import lax
from jax.experimental import pallas as pl
from jax.experimental.pallas import tpu as pltpu
from jax.sharding import PartitionSpec as P

HALO = 8
PSF_SIGMAS = (0.75, 1.5, 3.0)
PSF_REACH = 16
MID = 5
LANES = 128
HALF = 64
MESH = pl.DeviceIdType.MESH
BF16 = jnp.bfloat16
F32 = jnp.float32


def gaussian_taps(sigma, reach):
    distance = np.arange(-reach, reach + 1, dtype=np.float64)
    return np.exp(-distance * distance / (2.0 * sigma * sigma)) / (math.pi * sigma * sigma) ** 0.25


def well_rounded_scale(sigma, reach):
    taps = gaussian_taps(sigma, reach)
    scales = 1.0 + np.arange(1024) / 1024.0
    scaled = taps[None, :] * scales[:, None]
    rounded = scaled.astype(np.float32).astype(BF16).astype(np.float64)
    error = np.sum((rounded - scaled) ** 2, axis=1) / scales**2
    gain = (np.sum(rounded - scaled, axis=1) / scales) ** 2
    return float(scales[np.argmin(error + gain)])


def gaussian(distance, sigma, reach, scale):
    distance = distance.astype(F32)
    shape = jnp.exp(distance * distance * (-0.5 / (sigma * sigma))) * (scale / (math.pi * sigma * sigma) ** 0.25)
    return jnp.where(jnp.abs(distance) <= reach, shape, 0.0)


def row_minus_col(shape):
    return lax.broadcasted_iota(jnp.int32, shape, 0) - lax.broadcasted_iota(jnp.int32, shape, 1)


def split_high_low(matrix):
    high = matrix.astype(BF16)
    return high, (matrix - high.astype(F32)).astype(BF16)


def sinc(value):
    angle = jnp.where(value == 0.0, 1.0, math.pi * value)
    return jnp.where(value == 0.0, 1.0, jnp.sin(angle) / angle)


def lanczos(value):
    inside = jnp.abs(value) < 3.0
    value = jnp.where(inside, value, 0.0)
    return jnp.where(inside, sinc(value) * sinc(value / 3.0), 0.0)


LOW, HIGH = HALF - 16, HALF + LANES + 16


def column_warp(tile, table_row):
    rows, cols = tile.shape
    shape = (HIGH - LOW, LANES)
    band = pltpu.roll(jnp.broadcast_to(table_row, shape), 0, axis=1, stride=1, stride_axis=0)
    distance = row_minus_col(shape) - (HALF - LOW)
    band = jnp.where(jnp.abs(distance) <= MID, band, 0.0).astype(BF16)
    matrix = jnp.concatenate([jnp.zeros((LOW, LANES), BF16), band, jnp.zeros((2 * LANES - HIGH, LANES), BF16)], axis=0)
    edge = jnp.zeros((rows, LANES), BF16)
    padded = jnp.concatenate([edge, tile, edge], axis=1)
    blocks = cols // LANES + 1
    windows = jnp.concatenate([padded[:, m * LANES : (m + 2) * LANES] for m in range(blocks)], axis=0)
    return jnp.dot(windows, matrix, preferred_element_type=F32).astype(BF16)


def row_matrices(table_rows, factors, g_rows, rows):
    shape = (rows, LANES)
    per = LANES // rows
    lane_slot = lax.broadcasted_iota(jnp.int32, shape, 1) // rows
    shifts = []
    for first in range(0, len(table_rows), per):
        both = jnp.zeros(shape, F32)
        for s in range(per):
            row = jnp.broadcast_to(table_rows[first + s], shape)
            band = pltpu.roll(row, s * rows, axis=1, stride=1, stride_axis=0)
            both = jnp.where(lane_slot == s, band, both)
        shifts.append(both.astype(BF16))
    shift = jnp.concatenate(shifts, axis=1)
    blurred = jnp.dot(g_rows, jnp.concatenate([shift, shift], axis=0), preferred_element_type=F32)
    pieces = []
    for k in range(3):
        factor = factors[k : k + 1, :] + factors[3 + k : 4 + k, :]
        pieces.append(blurred[k * rows : (k + 1) * rows] * factor)
    return jnp.concatenate(pieces, axis=0).astype(BF16)


def detect(coadd, before, after):
    rows, cols = coadd.shape
    sigma = HALO / 4.0
    scale = well_rounded_scale(sigma, HALO)
    extended = jnp.concatenate([before, coadd, after], axis=0)
    h_rows = gaussian(row_minus_col((rows, rows + 2 * HALO)) + HALO, sigma, HALO, 1.0 / scale)
    blurred = jnp.dot(h_rows, extended, preferred_element_type=F32, precision=lax.Precision.HIGHEST).astype(BF16)
    h_cols = gaussian(row_minus_col((3 * LANES, LANES)) - LANES, sigma, HALO, scale).astype(BF16)
    edge = jnp.zeros((rows, LANES), BF16)
    padded = jnp.concatenate([edge, blurred, edge], axis=1)
    windows = jnp.concatenate([padded[:, m * LANES : (m + 3) * LANES] for m in range(cols // LANES)], axis=0)
    result = jnp.dot(windows, h_cols, preferred_element_type=F32)
    return jnp.concatenate([result[m * rows : (m + 1) * rows] for m in range(cols // LANES)], axis=1)


def slot_tables(named, offsets, coefs, weights, owners, capacity):
    count = named.shape[1]
    slots = owners * capacity
    square = (count, count)
    sublane, lane = lax.broadcasted_iota(jnp.int32, square, 0), lax.broadcasted_iota(jnp.int32, square, 1)

    def to_column(row):
        spread = jnp.where(sublane == lane, jnp.broadcast_to(row, square), jnp.zeros(square, row.dtype))
        return jnp.sum(spread, axis=1, keepdims=True)

    named_column = to_column(named)
    same = jnp.where(jnp.broadcast_to(named, square) == jnp.broadcast_to(named_column, square), 1, 0)
    rank_row = jnp.sum(jnp.where(sublane < lane, same, 0), axis=0, keepdims=True)
    rank_column = jnp.sum(jnp.where(lane < sublane, same, 0), axis=1, keepdims=True)
    slot_row = named * capacity + rank_row
    slot_column = named_column * capacity + rank_column

    chosen = lax.broadcasted_iota(jnp.int32, (slots, count), 0) == slot_row
    place = lax.broadcasted_iota(jnp.int32, (count, slots), 1) == slot_column
    tile = lax.broadcasted_iota(jnp.int32, (count, slots), 0)
    source = jnp.sum(jnp.where(place, tile, 0), axis=0, keepdims=True)

    shift = offsets.astype(F32) / 64.0
    at = lax.broadcasted_iota(jnp.int32, (count, LANES), 1)
    col_table = lanczos((at - LANES + HALF - LOW).astype(F32) + to_column(shift[1:2]))
    col_table = col_table.astype(BF16).astype(F32)
    row_table = lanczos(jnp.where(at < HALF, -at, LANES - at).astype(F32) + to_column(shift[0:1]))
    one = jnp.where(chosen, 1.0, 0.0).astype(BF16)
    row_table = jnp.dot(one, row_table.astype(BF16), preferred_element_type=F32)
    factor = weights * (coefs.astype(F32) / 64.0)
    high, low = split_high_low(factor)
    rest = jnp.zeros((2, count), F32)
    factors = jnp.concatenate([high.astype(F32), low.astype(F32), rest], axis=0).astype(BF16)
    return col_table, row_table, factors, slot_column, source


def fused_kernel(
    owners, capacity, chunk,
    tiles_hbm, args_ref, weight_ref,
    coadd_ref, detection_ref,
    tiles, warped, blur, part, g_rows, g_cols, load_sems,
    col_table, row_table, factor_rows, slot_column, w_part, source_row, source, source_sem,
    pair_in, sums, cross_in, arrived, w_pair, w_sums, w_arrived, halos,
    pair_send, pair_recv, w_pair_sems, cross_send, cross_recv, send, recv, w_send, w_recv,
    last_sems, halo_send, halo_recv,
):
    me, core = lax.axis_index("patch"), lax.axis_index("visit")
    other = 1 - core
    duos = owners // 2
    duo, side = me // 2, me % 2
    count, rows, cols = tiles.shape
    wide = cols + LANES
    half = rows // 2
    chunks = count // chunk
    mine, theirs = pl.ds(core * half, half), pl.ds(other * half, half)

    def load(c):
        span = pl.ds(c * chunk, chunk)
        return pltpu.make_async_copy(tiles_hbm.at[span], tiles.at[span], load_sems.at[c])

    for c in range(chunks):
        load(c).start()

    barrier = pltpu.get_barrier_semaphore()

    def greet(i, carry):
        flat = (me * 2 + core + i) % (2 * owners)
        pl.semaphore_signal(barrier, inc=1, device_id={"patch": flat // 2, "visit": flat % 2}, device_id_type=MESH)
        return carry

    lax.fori_loop(1, 2 * owners, greet, 0)

    for k, sigma in enumerate(PSF_SIGMAS):
        scale = well_rounded_scale(sigma, PSF_REACH)
        high, low = split_high_low(gaussian(row_minus_col((rows, rows)), sigma, PSF_REACH, 1.0 / scale))
        g_rows[k * rows : (k + 1) * rows] = jnp.concatenate([high, low], axis=1)
        taps = gaussian(row_minus_col((2 * LANES, LANES)) - HALF, sigma, PSF_REACH, scale)
        g_cols[2 * k * LANES : 2 * (k + 1) * LANES] = taps.astype(BF16)

    args = args_ref[...]
    named, weight = args[0:1], weight_ref[...]
    col_values, row_values, factor_values, column, row = slot_tables(
        named, args[1:3], args[3:6], weight, owners, capacity
    )
    source_row[...] = row
    source_copy = pltpu.make_async_copy(source_row, source, source_sem)
    source_copy.start()
    col_table[...] = col_values
    row_table[...] = row_values
    factor_rows[...] = factor_values
    slot_column[...] = column
    for p in range(owners):
        here = jnp.where(named == p, weight * weight, 0.0)
        w_part[p] = jnp.broadcast_to(jnp.sum(here, axis=1, keepdims=True), (8, LANES))

    def warp_chunk(c, carry):
        load(c).wait()

        def warp(step, carry):
            v = c * chunk + step
            result = column_warp(tiles[v], col_table[pl.ds(v, 1), :])
            for m in range(wide // LANES):
                warped[v, :, m * LANES : (m + 1) * LANES] = result[m * rows : (m + 1) * rows]
            return carry

        return lax.fori_loop(0, chunk, warp, carry, unroll=4 if chunk % 4 == 0 else 1)

    lax.fori_loop(0, chunks, warp_chunk, 0)
    source_copy.wait()

    pl.semaphore_wait(barrier, 2 * owners - 1)

    def pair_copy(q):
        return pltpu.make_async_remote_copy(
            part.at[q, theirs], pair_in.at[q], pair_send.at[q], pair_recv.at[q],
            device_id={"visit": other}, device_id_type=MESH,
        )

    w_copy = pltpu.make_async_remote_copy(
        w_part, w_pair, w_pair_sems.at[0], w_pair_sems.at[1], device_id={"visit": other}, device_id_type=MESH
    )

    def cross_copy(g):
        return pltpu.make_async_remote_copy(
            sums.at[2 * g + 1 - side], cross_in.at[g], cross_send.at[g], cross_recv.at[g],
            device_id={"patch": 2 * duo + 1 - side}, device_id_type=MESH,
        )

    def out_copy(g, slot):
        return pltpu.make_async_remote_copy(
            sums.at[2 * g + side], arrived.at[slot], send.at[g], recv.at[slot],
            device_id={"patch": 2 * g + side}, device_id_type=MESH,
        )

    def w_out_copy(q, slot):
        return pltpu.make_async_remote_copy(
            w_sums.at[q], w_arrived.at[slot], w_send.at[q], w_recv.at[slot], device_id={"patch": q}, device_id_type=MESH
        )

    w_copy.start()

    depth = capacity * rows
    pieces = [(a, min(a + 2 * LANES, wide)) for a in range(0, wide, 2 * LANES)]

    def compute(p):
        lane_slot = p * capacity + lax.broadcasted_iota(jnp.int32, (count, depth), 1) // rows
        spread = jnp.where(slot_column[...] == lane_slot, 1.0, 0.0).astype(BF16)
        factors = jnp.dot(factor_rows[...], spread, preferred_element_type=F32)
        table_rows = [row_table[pl.ds(p * capacity + r, 1), :] for r in range(capacity)]
        left = row_matrices(table_rows, factors, g_rows[...], rows)
        slots = [jnp.clip(source[0, p * capacity + r], 0, count - 1) for r in range(capacity)]
        for a, b in pieces:
            right = jnp.concatenate([warped[s, :, a:b] for s in slots], axis=0)
            total = jnp.dot(left, right, preferred_element_type=F32)
            lane = a + lax.broadcasted_iota(jnp.int32, total.shape, 1)
            if a < HALF or b > wide - HALF:
                total = jnp.where((lane >= HALF) & (lane < wide - HALF), total, 0.0)
            blur[:, a:b] = total.astype(BF16)
        windows = jnp.concatenate(
            [
                jnp.concatenate([blur[k * rows : (k + 1) * rows, m * LANES : (m + 2) * LANES] for k in range(3)], axis=1)
                for m in range(cols // LANES)
            ],
            axis=0,
        )
        result = jnp.dot(windows, g_cols[...], preferred_element_type=F32).astype(BF16)
        for m in range(cols // LANES):
            part[p, :, m * LANES : (m + 1) * LANES] = result[m * rows : (m + 1) * rows]
        pair_copy(p).start()

    def core_sum(q):
        pair_copy(q).wait()
        return part[q, mine].astype(F32) + pair_in[q].astype(F32)

    def pass_across(g):
        q = 2 * g + 1 - side
        sums[q] = core_sum(q).astype(BF16)
        cross_copy(g).start()

    def duo_sum(g):
        total = core_sum(2 * g + side)
        cross_copy(g).wait_recv()
        return total + cross_in[g].astype(F32)

    def forward(g):
        sums[2 * g + side] = duo_sum(g).astype(BF16)
        out_copy(g, duo).start()

    first = (duo + 1) % duos
    compute(2 * first + 1 - side)
    w_copy.wait()
    w_sums[...] = w_part[...] + w_pair[...]

    def send_weight(i, carry):
        w_out_copy((me + i) % owners, me).start()
        return carry

    lax.fori_loop(1, owners, send_weight, 0)
    compute(2 * first + side)
    pass_across(first)

    def both_patches(i, carry):
        g = (duo + i) % duos
        compute(2 * g + 1 - side)
        forward((duo + i - 1) % duos)
        compute(2 * g + side)
        pass_across(g)
        return carry

    lax.fori_loop(2, duos + 1, both_patches, 0)
    total = duo_sum(duo)

    def collect(i, total):
        g = (duo + duos - i) % duos
        out_copy(g, g).wait_recv()
        return total + arrived[g].astype(F32)

    total = lax.fori_loop(1, duos, collect, total)

    def collect_weight(i, weight):
        q = (me + owners - i) % owners
        w_out_copy(q, q).wait_recv()
        return weight + w_arrived[q]

    weight = lax.fori_loop(1, owners, collect_weight, w_sums[me])
    coadd_ref[mine] = total / jnp.sqrt(weight[0:1, 0:1])

    last = pltpu.make_async_remote_copy(
        coadd_ref.at[mine], coadd_ref.at[mine], last_sems.at[0], last_sems.at[1],
        device_id={"visit": other}, device_id_type=MESH,
    )
    last.start()
    neighbour = (me + owners - 1 + 2 * core) % owners
    border = pl.ds(core * (rows - HALO), HALO)

    def halo_copy(to):
        return pltpu.make_async_remote_copy(
            coadd_ref.at[border], halos.at[other], halo_send.at[to], halo_recv.at[other],
            device_id={"patch": neighbour, "visit": to}, device_id_type=MESH,
        )

    for to in range(2):
        halo_copy(to).start()

    def finish_weight(i, carry):
        w_out_copy((me + i) % owners, me).wait_send()
        return carry

    def finish(i, carry):
        g = (duo + i) % duos
        cross_copy(g).wait_send()
        out_copy(g, duo).wait_send()
        return carry

    lax.fori_loop(1, owners, finish_weight, 0)
    lax.fori_loop(1, duos, finish, 0)
    cross_copy(duo).wait_send()
    for to in range(2):
        halo_copy(to).wait_send()
    for end in range(2):
        pltpu.make_async_remote_copy(
            coadd_ref.at[border], halos.at[end], halo_send.at[0], halo_recv.at[end],
            device_id={"patch": neighbour, "visit": other}, device_id_type=MESH,
        ).wait_recv()
    last.wait()
    before = jnp.where(me > 0, halos[0], 0.0)
    after = jnp.where(me < owners - 1, halos[1], 0.0)
    detection_ref[...] = detect(coadd_ref[...], before, after)


def shards(visit_tiles, tile_patch, offsets, psf_coefs, weights):
    count, rows, cols = visit_tiles.shape
    owners = lax.axis_size("patch")
    capacity = max(2, 2 * count // owners)
    capacity += capacity % 2
    chunk = math.gcd(count, 8)
    wide = cols + LANES
    half = rows // 2
    args, first = jnp.zeros((8, count), jnp.int32), 0
    for array in (tile_patch[None, :], offsets.T, psf_coefs.T):
        last = first + array.shape[0]
        args = args + jnp.pad(array, ((first, 8 - last), (0, 0)))
        first = last
    vmem = pl.BlockSpec(memory_space=pltpu.VMEM)
    hbm = pl.BlockSpec(memory_space=pltpu.HBM)
    dma = pltpu.SemaphoreType.DMA
    return pl.pallas_call(
        functools.partial(fused_kernel, owners, capacity, chunk),
        out_shape=(jax.ShapeDtypeStruct((rows, cols), F32), jax.ShapeDtypeStruct((rows, cols), F32)),
        in_specs=[hbm, vmem, vmem],
        out_specs=(vmem, vmem),
        scratch_shapes=[
            pltpu.VMEM((count, rows, cols), BF16),
            pltpu.VMEM((count, rows, wide), BF16),
            pltpu.VMEM((3 * rows, wide), BF16),
            pltpu.VMEM((owners, rows, cols), BF16),
            pltpu.VMEM((3 * rows, 2 * rows), BF16),
            pltpu.VMEM((6 * LANES, LANES), BF16),
            dma((count // chunk,)),
            pltpu.VMEM((count, LANES), F32),
            pltpu.VMEM((owners * capacity, LANES), F32),
            pltpu.VMEM((8, count), BF16),
            pltpu.VMEM((count, 1), jnp.int32),
            pltpu.VMEM((owners, 8, LANES), F32),
            pltpu.VMEM((1, owners * capacity), jnp.int32),
            pltpu.SMEM((1, owners * capacity), jnp.int32),
            dma(()),
            pltpu.VMEM((owners, half, cols), BF16),
            pltpu.VMEM((owners, half, cols), BF16),
            pltpu.VMEM((owners // 2, half, cols), BF16),
            pltpu.VMEM((owners // 2, half, cols), BF16),
            pltpu.VMEM((owners, 8, LANES), F32),
            pltpu.VMEM((owners, 8, LANES), F32),
            pltpu.VMEM((owners, 8, LANES), F32),
            pltpu.VMEM((2, HALO, cols), F32),
            dma((owners,)), dma((owners,)), dma((2,)),
            dma((owners // 2,)), dma((owners // 2,)), dma((owners // 2,)), dma((owners // 2,)),
            dma((owners,)), dma((owners,)),
            dma((2,)), dma((2,)), dma((2,)),
        ],
        compiler_params=pltpu.CompilerParams(
            collective_id=0, has_side_effects=True, vmem_limit_bytes=52 * 2**20
        ),
        name="fused",
    )(visit_tiles, args, weights.astype(F32)[None, :])


def solution(mesh):
    placed = (
        P(("groups", "patch", "visit"), None, None),
        P(("groups", "patch", "visit")),
        P(("groups", "patch", "visit"), None),
        P(("groups", "patch", "visit"), None),
        P(("groups", "patch", "visit")),
    )
    return jax.shard_map(
        shards,
        mesh=mesh,
        in_specs=placed,
        out_specs=(P(("groups", "patch"), None), P(("groups", "patch"), None)),
        check_vma=False,
    )
```

```python
import functools
import math

import jax
import jax.numpy as jnp
import numpy as np
from jax import lax
from jax.experimental import pallas as pl
from jax.experimental.pallas import tpu as pltpu
from jax.sharding import PartitionSpec as P

HALO = 8
PSF_SIGMAS = (0.75, 1.5, 3.0)
PSF_REACH = 16
MID = 5
LANES = 128
HALF = 64
MESH = pl.DeviceIdType.MESH
BF16 = jnp.bfloat16
F32 = jnp.float32


def gaussian_taps(sigma, reach):
    distance = np.arange(-reach, reach + 1, dtype=np.float64)
    return np.exp(-distance * distance / (2.0 * sigma * sigma)) / (math.pi * sigma * sigma) ** 0.25


def well_rounded_scale(sigma, reach):
    taps = gaussian_taps(sigma, reach)
    scales = 1.0 + np.arange(1024) / 1024.0
    scaled = taps[None, :] * scales[:, None]
    rounded = scaled.astype(np.float32).astype(BF16).astype(np.float64)
    error = np.sum((rounded - scaled) ** 2, axis=1) / scales**2
    gain = (np.sum(rounded - scaled, axis=1) / scales) ** 2
    return float(scales[np.argmin(error + gain)])


def gaussian(distance, sigma, reach, scale):
    distance = distance.astype(F32)
    shape = jnp.exp(distance * distance * (-0.5 / (sigma * sigma))) * (scale / (math.pi * sigma * sigma) ** 0.25)
    return jnp.where(jnp.abs(distance) <= reach, shape, 0.0)


def row_minus_col(shape):
    return lax.broadcasted_iota(jnp.int32, shape, 0) - lax.broadcasted_iota(jnp.int32, shape, 1)


def split_high_low(matrix):
    high = matrix.astype(BF16)
    return high, (matrix - high.astype(F32)).astype(BF16)


def sinc(value):
    angle = jnp.where(value == 0.0, 1.0, math.pi * value)
    return jnp.where(value == 0.0, 1.0, jnp.sin(angle) / angle)


def lanczos(value):
    inside = jnp.abs(value) < 3.0
    value = jnp.where(inside, value, 0.0)
    return jnp.where(inside, sinc(value) * sinc(value / 3.0), 0.0)


LOW, HIGH = HALF - 16, HALF + LANES + 16


def column_warp(tile, table_row):
    rows, cols = tile.shape
    shape = (HIGH - LOW, LANES)
    band = pltpu.roll(jnp.broadcast_to(table_row, shape), 0, axis=1, stride=1, stride_axis=0)
    distance = row_minus_col(shape) - (HALF - LOW)
    band = jnp.where(jnp.abs(distance) <= MID, band, 0.0).astype(BF16)
    matrix = jnp.concatenate([jnp.zeros((LOW, LANES), BF16), band, jnp.zeros((2 * LANES - HIGH, LANES), BF16)], axis=0)
    edge = jnp.zeros((rows, LANES), BF16)
    padded = jnp.concatenate([edge, tile, edge], axis=1)
    blocks = cols // LANES + 1
    windows = jnp.concatenate([padded[:, m * LANES : (m + 2) * LANES] for m in range(blocks)], axis=0)
    return jnp.dot(windows, matrix, preferred_element_type=F32).astype(BF16)


def row_matrices(table_rows, factors, g_rows, rows):
    shape = (rows, LANES)
    per = LANES // rows
    lane_slot = lax.broadcasted_iota(jnp.int32, shape, 1) // rows
    shifts = []
    for first in range(0, len(table_rows), per):
        both = jnp.zeros(shape, F32)
        for s in range(per):
            row = jnp.broadcast_to(table_rows[first + s], shape)
            band = pltpu.roll(row, s * rows, axis=1, stride=1, stride_axis=0)
            both = jnp.where(lane_slot == s, band, both)
        shifts.append(both.astype(BF16))
    shift = jnp.concatenate(shifts, axis=1)
    blurred = jnp.dot(g_rows, jnp.concatenate([shift, shift], axis=0), preferred_element_type=F32)
    pieces = []
    for k in range(3):
        factor = factors[k : k + 1, :] + factors[3 + k : 4 + k, :]
        pieces.append(blurred[k * rows : (k + 1) * rows] * factor)
    return jnp.concatenate(pieces, axis=0).astype(BF16)


def detect(coadd, before, after):
    rows, cols = coadd.shape
    sigma = HALO / 4.0
    scale = well_rounded_scale(sigma, HALO)
    extended = jnp.concatenate([before, coadd, after], axis=0)
    h_rows = gaussian(row_minus_col((rows, rows + 2 * HALO)) + HALO, sigma, HALO, 1.0 / scale)
    blurred = jnp.dot(h_rows, extended, preferred_element_type=F32, precision=lax.Precision.HIGHEST).astype(BF16)
    h_cols = gaussian(row_minus_col((3 * LANES, LANES)) - LANES, sigma, HALO, scale).astype(BF16)
    edge = jnp.zeros((rows, LANES), BF16)
    padded = jnp.concatenate([edge, blurred, edge], axis=1)
    windows = jnp.concatenate([padded[:, m * LANES : (m + 3) * LANES] for m in range(cols // LANES)], axis=0)
    result = jnp.dot(windows, h_cols, preferred_element_type=F32)
    return jnp.concatenate([result[m * rows : (m + 1) * rows] for m in range(cols // LANES)], axis=1)


def slot_tables(named, offsets, coefs, weights, owners, capacity):
    count = named.shape[1]
    slots = owners * capacity
    square = (count, count)
    sublane, lane = lax.broadcasted_iota(jnp.int32, square, 0), lax.broadcasted_iota(jnp.int32, square, 1)

    def to_column(row):
        spread = jnp.where(sublane == lane, jnp.broadcast_to(row, square), jnp.zeros(square, row.dtype))
        return jnp.sum(spread, axis=1, keepdims=True)

    named_column = to_column(named)
    same = jnp.where(jnp.broadcast_to(named, square) == jnp.broadcast_to(named_column, square), 1, 0)
    rank_row = jnp.sum(jnp.where(sublane < lane, same, 0), axis=0, keepdims=True)
    rank_column = jnp.sum(jnp.where(lane < sublane, same, 0), axis=1, keepdims=True)
    slot_row = named * capacity + rank_row
    slot_column = named_column * capacity + rank_column

    chosen = lax.broadcasted_iota(jnp.int32, (slots, count), 0) == slot_row
    place = lax.broadcasted_iota(jnp.int32, (count, slots), 1) == slot_column
    tile = lax.broadcasted_iota(jnp.int32, (count, slots), 0)
    source = jnp.sum(jnp.where(place, tile, 0), axis=0, keepdims=True)

    shift = offsets.astype(F32) / 64.0
    at = lax.broadcasted_iota(jnp.int32, (count, LANES), 1)
    col_table = lanczos((at - LANES + HALF - LOW).astype(F32) + to_column(shift[1:2]))
    col_table = col_table.astype(BF16).astype(F32)
    row_table = lanczos(jnp.where(at < HALF, -at, LANES - at).astype(F32) + to_column(shift[0:1]))
    one = jnp.where(chosen, 1.0, 0.0).astype(BF16)
    row_table = jnp.dot(one, row_table.astype(BF16), preferred_element_type=F32)
    factor = weights * (coefs.astype(F32) / 64.0)
    high, low = split_high_low(factor)
    rest = jnp.zeros((2, count), F32)
    factors = jnp.concatenate([high.astype(F32), low.astype(F32), rest], axis=0).astype(BF16)
    return col_table, row_table, factors, slot_column, source


def fused_kernel(
    owners, capacity, chunk,
    tiles_hbm, args_ref, weight_ref,
    coadd_ref, detection_ref,
    tiles, warped, blur_even, blur_odd, left_even, left_odd, part, g_rows, g_cols, load_sems,
    col_table, row_table, factor_rows, slot_column, w_part, source_row, source, source_sem,
    pair_in, sums, arrived, w_pair, w_sums, w_arrived, halos,
    pair_send, pair_recv, w_pair_sems, send, recv, w_send, w_recv, last_sems, halo_send, halo_recv,
):
    me, core = lax.axis_index("patch"), lax.axis_index("visit")
    other = 1 - core
    count, rows, cols = tiles.shape
    wide = cols + LANES
    half = rows // 2
    chunks = count // chunk
    mine, theirs = pl.ds(core * half, half), pl.ds(other * half, half)

    def load(c):
        span = pl.ds(c * chunk, chunk)
        return pltpu.make_async_copy(tiles_hbm.at[span], tiles.at[span], load_sems.at[c])

    for c in range(chunks):
        load(c).start()

    barrier = pltpu.get_barrier_semaphore()

    def greet(i, carry):
        flat = (me * 2 + core + i) % (2 * owners)
        pl.semaphore_signal(barrier, inc=1, device_id={"patch": flat // 2, "visit": flat % 2}, device_id_type=MESH)
        return carry

    lax.fori_loop(1, 2 * owners, greet, 0)

    for k, sigma in enumerate(PSF_SIGMAS):
        scale = well_rounded_scale(sigma, PSF_REACH)
        high, low = split_high_low(gaussian(row_minus_col((rows, rows)), sigma, PSF_REACH, 1.0 / scale))
        g_rows[k * rows : (k + 1) * rows] = jnp.concatenate([high, low], axis=1)
        taps = gaussian(row_minus_col((2 * LANES, LANES)) - HALF, sigma, PSF_REACH, scale)
        g_cols[2 * k * LANES : 2 * (k + 1) * LANES] = taps.astype(BF16)

    args = args_ref[...]
    named, weight = args[0:1], weight_ref[...]
    col_values, row_values, factor_values, column, row = slot_tables(
        named, args[1:3], args[3:6], weight, owners, capacity
    )
    source_row[...] = row
    source_copy = pltpu.make_async_copy(source_row, source, source_sem)
    source_copy.start()
    col_table[...] = col_values
    row_table[...] = row_values
    factor_rows[...] = factor_values
    slot_column[...] = column
    for p in range(owners):
        here = jnp.where(named == p, weight * weight, 0.0)
        w_part[p] = jnp.broadcast_to(jnp.sum(here, axis=1, keepdims=True), (8, LANES))

    def warp_chunk(c, carry):
        load(c).wait()

        def warp(step, carry):
            v = c * chunk + step
            result = column_warp(tiles[v], col_table[pl.ds(v, 1), :])
            for m in range(wide // LANES):
                warped[v, :, m * LANES : (m + 1) * LANES] = result[m * rows : (m + 1) * rows]
            return carry

        return lax.fori_loop(0, chunk, warp, carry, unroll=chunk)

    lax.fori_loop(0, chunks, warp_chunk, 0)
    source_copy.wait()

    pl.semaphore_wait(barrier, 2 * owners - 1)

    def pair_copy(q):
        return pltpu.make_async_remote_copy(
            part.at[q, theirs], pair_in.at[q], pair_send.at[q], pair_recv.at[q],
            device_id={"visit": other}, device_id_type=MESH,
        )

    w_copy = pltpu.make_async_remote_copy(
        w_part, w_pair, w_pair_sems.at[0], w_pair_sems.at[1], device_id={"visit": other}, device_id_type=MESH
    )

    def out_copy(q, slot):
        return pltpu.make_async_remote_copy(
            sums.at[q], arrived.at[slot], send.at[q], recv.at[slot], device_id={"patch": q}, device_id_type=MESH
        )

    def w_out_copy(q, slot):
        return pltpu.make_async_remote_copy(
            w_sums.at[q], w_arrived.at[slot], w_send.at[q], w_recv.at[slot], device_id={"patch": q}, device_id_type=MESH
        )

    w_copy.start()

    depth = capacity * rows
    pieces = [(a, min(a + 2 * LANES, wide)) for a in range(0, wide, 2 * LANES)]

    lefts, blurs = (left_even, left_odd), (blur_even, blur_odd)

    def owner(i):
        return (me + i) % owners

    def prepare(i, parity):
        p = owner(i)
        lane_slot = p * capacity + lax.broadcasted_iota(jnp.int32, (count, depth), 1) // rows
        spread = jnp.where(slot_column[...] == lane_slot, 1.0, 0.0).astype(BF16)
        factors = jnp.dot(factor_rows[...], spread, preferred_element_type=F32)
        table_rows = [row_table[pl.ds(p * capacity + r, 1), :] for r in range(capacity)]
        lefts[parity][...] = row_matrices(table_rows, factors, g_rows[...], rows)

    def stack(i, parity):
        p = owner(i)
        slots = [jnp.clip(source[0, p * capacity + r], 0, count - 1) for r in range(capacity)]
        for a, b in pieces:
            right = jnp.concatenate([warped[s, :, a:b] for s in slots], axis=0)
            total = jnp.dot(lefts[parity][...], right, preferred_element_type=F32)
            lane = a + lax.broadcasted_iota(jnp.int32, total.shape, 1)
            if a < HALF or b > wide - HALF:
                total = jnp.where((lane >= HALF) & (lane < wide - HALF), total, 0.0)
            blurs[parity][:, a:b] = total.astype(BF16)

    def match(i, parity):
        p, blur = owner(i), blurs[parity]
        windows = jnp.concatenate(
            [
                jnp.concatenate([blur[k * rows : (k + 1) * rows, m * LANES : (m + 2) * LANES] for k in range(3)], axis=1)
                for m in range(cols // LANES)
            ],
            axis=0,
        )
        result = jnp.dot(windows, g_cols[...], preferred_element_type=F32).astype(BF16)
        for m in range(cols // LANES):
            part[p, :, m * LANES : (m + 1) * LANES] = result[m * rows : (m + 1) * rows]

    def forward(q):
        pair_copy(q).wait()
        sums[q] = (part[q, mine].astype(F32) + pair_in[q].astype(F32)).astype(BF16)
        out_copy(q, me).start()
        w_out_copy(q, me).start()

    prepare(1, 1)
    prepare(2, 0)
    stack(1, 1)
    w_copy.wait()
    w_sums[...] = w_part[...] + w_pair[...]

    def step(i, parity):
        prepare(i + 1, 1 - parity)
        match(i - 1, 1 - parity)
        stack(i, parity)
        pair_copy(owner(i - 1)).start()

    step(2, 0)

    def two_patches(j, carry):
        step(2 * j + 1, 1)
        forward(owner(2 * j - 1))
        step(2 * j + 2, 0)
        forward(owner(2 * j))
        return carry

    lax.fori_loop(1, owners // 2, two_patches, 0)
    match(owners, 0)
    pair_copy(me).start()
    forward(owner(owners - 1))
    pair_copy(me).wait()
    total = part[me, mine].astype(F32) + pair_in[me].astype(F32)

    def collect(i, carry):
        total, weight = carry
        q = (me + owners - i) % owners
        out_copy(q, q).wait_recv()
        w_out_copy(q, q).wait_recv()
        return total + arrived[q].astype(F32), weight + w_arrived[q]

    total, weight = lax.fori_loop(1, owners, collect, (total, w_sums[me]))
    coadd_ref[mine] = total / jnp.sqrt(weight[0:1, 0:1])

    last = pltpu.make_async_remote_copy(
        coadd_ref.at[mine], coadd_ref.at[mine], last_sems.at[0], last_sems.at[1],
        device_id={"visit": other}, device_id_type=MESH,
    )
    last.start()
    neighbour = (me + owners - 1 + 2 * core) % owners
    border = pl.ds(core * (rows - HALO), HALO)

    def halo_copy(to):
        return pltpu.make_async_remote_copy(
            coadd_ref.at[border], halos.at[other], halo_send.at[to], halo_recv.at[other],
            device_id={"patch": neighbour, "visit": to}, device_id_type=MESH,
        )

    for to in range(2):
        halo_copy(to).start()

    def finish(i, carry):
        q = (me + i) % owners
        out_copy(q, me).wait_send()
        w_out_copy(q, me).wait_send()
        return carry

    lax.fori_loop(1, owners, finish, 0)
    for to in range(2):
        halo_copy(to).wait_send()
    for side in range(2):
        pltpu.make_async_remote_copy(
            coadd_ref.at[border], halos.at[side], halo_send.at[0], halo_recv.at[side],
            device_id={"patch": neighbour, "visit": other}, device_id_type=MESH,
        ).wait_recv()
    last.wait()
    before = jnp.where(me > 0, halos[0], 0.0)
    after = jnp.where(me < owners - 1, halos[1], 0.0)
    detection_ref[...] = detect(coadd_ref[...], before, after)


def shards(visit_tiles, tile_patch, offsets, psf_coefs, weights):
    count, rows, cols = visit_tiles.shape
    owners = lax.axis_size("patch")
    capacity = max(2, 2 * count // owners)
    capacity += capacity % 2
    chunk = math.gcd(count, 8)
    wide = cols + LANES
    half = rows // 2
    args, first = jnp.zeros((8, count), jnp.int32), 0
    for array in (tile_patch[None, :], offsets.T, psf_coefs.T):
        last = first + array.shape[0]
        args = args + jnp.pad(array, ((first, 8 - last), (0, 0)))
        first = last
    vmem = pl.BlockSpec(memory_space=pltpu.VMEM)
    hbm = pl.BlockSpec(memory_space=pltpu.HBM)
    dma = pltpu.SemaphoreType.DMA
    return pl.pallas_call(
        functools.partial(fused_kernel, owners, capacity, chunk),
        out_shape=(jax.ShapeDtypeStruct((rows, cols), F32), jax.ShapeDtypeStruct((rows, cols), F32)),
        in_specs=[hbm, vmem, vmem],
        out_specs=(vmem, vmem),
        scratch_shapes=[
            pltpu.VMEM((count, rows, cols), BF16),
            pltpu.VMEM((count, rows, wide), BF16),
            pltpu.VMEM((3 * rows, wide), BF16),
            pltpu.VMEM((3 * rows, wide), BF16),
            pltpu.VMEM((3 * rows, capacity * rows), BF16),
            pltpu.VMEM((3 * rows, capacity * rows), BF16),
            pltpu.VMEM((owners, rows, cols), BF16),
            pltpu.VMEM((3 * rows, 2 * rows), BF16),
            pltpu.VMEM((6 * LANES, LANES), BF16),
            dma((count // chunk,)),
            pltpu.VMEM((count, LANES), F32),
            pltpu.VMEM((owners * capacity, LANES), F32),
            pltpu.VMEM((8, count), BF16),
            pltpu.VMEM((count, 1), jnp.int32),
            pltpu.VMEM((owners, 8, LANES), F32),
            pltpu.VMEM((1, owners * capacity), jnp.int32),
            pltpu.SMEM((1, owners * capacity), jnp.int32),
            dma(()),
            pltpu.VMEM((owners, half, cols), BF16),
            pltpu.VMEM((owners, half, cols), BF16),
            pltpu.VMEM((owners, half, cols), BF16),
            pltpu.VMEM((owners, 8, LANES), F32),
            pltpu.VMEM((owners, 8, LANES), F32),
            pltpu.VMEM((owners, 8, LANES), F32),
            pltpu.VMEM((2, HALO, cols), F32),
            dma((owners,)), dma((owners,)), dma((2,)),
            dma((owners,)), dma((owners,)), dma((owners,)), dma((owners,)),
            dma((2,)), dma((2,)), dma((2,)),
        ],
        compiler_params=pltpu.CompilerParams(
            collective_id=0, has_side_effects=True, vmem_limit_bytes=52 * 2**20
        ),
        name="fused",
    )(visit_tiles, args, weights.astype(F32)[None, :])


def solution(mesh):
    placed = (
        P(("groups", "patch", "visit"), None, None),
        P(("groups", "patch", "visit")),
        P(("groups", "patch", "visit"), None),
        P(("groups", "patch", "visit"), None),
        P(("groups", "patch", "visit")),
    )
    return jax.shard_map(
        shards,
        mesh=mesh,
        in_specs=placed,
        out_specs=(P(("groups", "patch"), None), P(("groups", "patch"), None)),
        check_vma=False,
    )
```

```python
import functools
import math

import jax
import jax.numpy as jnp
import numpy as np
from jax import lax
from jax.experimental import pallas as pl
from jax.experimental.pallas import tpu as pltpu
from jax.sharding import PartitionSpec as P

HALO = 8
PSF_SIGMAS = (0.75, 1.5, 3.0)
PSF_REACH = 16
MID = 5
LANES = 128
HALF = 64
MESH = pl.DeviceIdType.MESH
BF16 = jnp.bfloat16
F32 = jnp.float32


def gaussian_taps(sigma, reach):
    distance = np.arange(-reach, reach + 1, dtype=np.float64)
    return np.exp(-distance * distance / (2.0 * sigma * sigma)) / (math.pi * sigma * sigma) ** 0.25


def well_rounded_scale(sigma, reach):
    taps = gaussian_taps(sigma, reach)
    scales = 1.0 + np.arange(1024) / 1024.0
    scaled = taps[None, :] * scales[:, None]
    rounded = scaled.astype(np.float32).astype(BF16).astype(np.float64)
    error = np.sum((rounded - scaled) ** 2, axis=1) / scales**2
    gain = (np.sum(rounded - scaled, axis=1) / scales) ** 2
    return float(scales[np.argmin(error + gain)])


def gaussian(distance, sigma, reach, scale):
    distance = distance.astype(F32)
    shape = jnp.exp(distance * distance * (-0.5 / (sigma * sigma))) * (scale / (math.pi * sigma * sigma) ** 0.25)
    return jnp.where(jnp.abs(distance) <= reach, shape, 0.0)


def row_minus_col(shape):
    return lax.broadcasted_iota(jnp.int32, shape, 0) - lax.broadcasted_iota(jnp.int32, shape, 1)


def split_high_low(matrix):
    high = matrix.astype(BF16)
    return high, (matrix - high.astype(F32)).astype(BF16)


def sinc(value):
    angle = jnp.where(value == 0.0, 1.0, math.pi * value)
    return jnp.where(value == 0.0, 1.0, jnp.sin(angle) / angle)


def lanczos(value):
    inside = jnp.abs(value) < 3.0
    value = jnp.where(inside, value, 0.0)
    return jnp.where(inside, sinc(value) * sinc(value / 3.0), 0.0)


LOW, HIGH = HALF - 16, HALF + LANES + 16


def column_warp(tile, table_row):
    rows, cols = tile.shape
    shape = (HIGH - LOW, LANES)
    band = pltpu.roll(jnp.broadcast_to(table_row, shape), 0, axis=1, stride=1, stride_axis=0)
    distance = row_minus_col(shape) - (HALF - LOW)
    band = jnp.where(jnp.abs(distance) <= MID, band, 0.0).astype(BF16)
    matrix = jnp.concatenate([jnp.zeros((LOW, LANES), BF16), band, jnp.zeros((2 * LANES - HIGH, LANES), BF16)], axis=0)
    edge = jnp.zeros((rows, LANES), BF16)
    padded = jnp.concatenate([edge, tile, edge], axis=1)
    blocks = cols // LANES + 1
    windows = jnp.concatenate([padded[:, m * LANES : (m + 2) * LANES] for m in range(blocks)], axis=0)
    return jnp.dot(windows, matrix, preferred_element_type=F32).astype(BF16)


def row_matrices(table_rows, factors, g_rows, rows):
    shape = (rows, LANES)
    per = LANES // rows
    lane_slot = lax.broadcasted_iota(jnp.int32, shape, 1) // rows
    shifts = []
    for first in range(0, len(table_rows), per):
        both = jnp.zeros(shape, F32)
        for s in range(per):
            row = jnp.broadcast_to(table_rows[first + s], shape)
            band = pltpu.roll(row, s * rows, axis=1, stride=1, stride_axis=0)
            both = jnp.where(lane_slot == s, band, both)
        shifts.append(both.astype(BF16))
    shift = jnp.concatenate(shifts, axis=1)
    blurred = jnp.dot(g_rows, jnp.concatenate([shift, shift], axis=0), preferred_element_type=F32)
    pieces = []
    for k in range(3):
        factor = factors[k : k + 1, :] + factors[3 + k : 4 + k, :]
        pieces.append(blurred[k * rows : (k + 1) * rows] * factor)
    return jnp.concatenate(pieces, axis=0).astype(BF16)


def detect(coadd, before, after):
    rows, cols = coadd.shape
    sigma = HALO / 4.0
    scale = well_rounded_scale(sigma, HALO)
    extended = jnp.concatenate([before, coadd, after], axis=0)
    h_rows = gaussian(row_minus_col((rows, rows + 2 * HALO)) + HALO, sigma, HALO, 1.0 / scale)
    blurred = jnp.dot(h_rows, extended, preferred_element_type=F32, precision=lax.Precision.HIGHEST).astype(BF16)
    h_cols = gaussian(row_minus_col((3 * LANES, LANES)) - LANES, sigma, HALO, scale).astype(BF16)
    edge = jnp.zeros((rows, LANES), BF16)
    padded = jnp.concatenate([edge, blurred, edge], axis=1)
    windows = jnp.concatenate([padded[:, m * LANES : (m + 3) * LANES] for m in range(cols // LANES)], axis=0)
    result = jnp.dot(windows, h_cols, preferred_element_type=F32)
    return jnp.concatenate([result[m * rows : (m + 1) * rows] for m in range(cols // LANES)], axis=1)


def slot_tables(named, offsets, coefs, weights, owners, capacity):
    count = named.shape[1]
    slots = owners * capacity
    square = (count, count)
    sublane, lane = lax.broadcasted_iota(jnp.int32, square, 0), lax.broadcasted_iota(jnp.int32, square, 1)

    def to_column(row):
        spread = jnp.where(sublane == lane, jnp.broadcast_to(row, square), jnp.zeros(square, row.dtype))
        return jnp.sum(spread, axis=1, keepdims=True)

    named_column = to_column(named)
    same = jnp.where(jnp.broadcast_to(named, square) == jnp.broadcast_to(named_column, square), 1, 0)
    rank_row = jnp.sum(jnp.where(sublane < lane, same, 0), axis=0, keepdims=True)
    rank_column = jnp.sum(jnp.where(lane < sublane, same, 0), axis=1, keepdims=True)
    slot_row = named * capacity + rank_row
    slot_column = named_column * capacity + rank_column

    chosen = lax.broadcasted_iota(jnp.int32, (slots, count), 0) == slot_row
    place = lax.broadcasted_iota(jnp.int32, (count, slots), 1) == slot_column
    tile = lax.broadcasted_iota(jnp.int32, (count, slots), 0)
    source = jnp.sum(jnp.where(place, tile, 0), axis=0, keepdims=True)

    shift = offsets.astype(F32) / 64.0
    at = lax.broadcasted_iota(jnp.int32, (count, LANES), 1)
    col_table = lanczos((at - LANES + HALF - LOW).astype(F32) + to_column(shift[1:2]))
    col_table = col_table.astype(BF16).astype(F32)
    row_table = lanczos(jnp.where(at < HALF, -at, LANES - at).astype(F32) + to_column(shift[0:1]))
    one = jnp.where(chosen, 1.0, 0.0).astype(BF16)
    row_table = jnp.dot(one, row_table.astype(BF16), preferred_element_type=F32)
    factor = weights * (coefs.astype(F32) / 64.0)
    high, low = split_high_low(factor)
    rest = jnp.zeros((2, count), F32)
    factors = jnp.concatenate([high.astype(F32), low.astype(F32), rest], axis=0).astype(BF16)
    return col_table, row_table, factors, slot_column, source


def fused_kernel(
    owners, capacity, chunk,
    tiles_hbm, args_ref, weight_ref,
    out_ref,
    tiles, warped, blur_even, blur_odd, left_even, left_odd, part, g_rows, g_cols, load_sems,
    col_table, row_table, factor_rows, slot_column, w_part, source_row, source, source_sem,
    pair_in, sums, arrived, w_pair, w_sums, w_arrived, halos,
    pair_send, pair_recv, w_pair_sems, send, recv, w_send, w_recv, last_sems, halo_send, halo_recv,
):
    me, core = lax.axis_index("patch"), lax.axis_index("visit")
    other = 1 - core
    count, rows, cols = tiles.shape
    wide = cols + LANES
    half = rows // 2
    chunks = count // chunk
    coadd_ref = out_ref.at[0]
    mine, theirs = pl.ds(core * half, half), pl.ds(other * half, half)

    def load(c):
        span = pl.ds(c * chunk, chunk)
        return pltpu.make_async_copy(tiles_hbm.at[span], tiles.at[span], load_sems.at[c])

    for c in range(chunks):
        load(c).start()

    barrier = pltpu.get_barrier_semaphore()

    def greet(i, carry):
        flat = (me * 2 + core + i) % (2 * owners)
        pl.semaphore_signal(barrier, inc=1, device_id={"patch": flat // 2, "visit": flat % 2}, device_id_type=MESH)
        return carry

    lax.fori_loop(1, 2 * owners, greet, 0)

    for k, sigma in enumerate(PSF_SIGMAS):
        scale = well_rounded_scale(sigma, PSF_REACH)
        high, low = split_high_low(gaussian(row_minus_col((rows, rows)), sigma, PSF_REACH, 1.0 / scale))
        g_rows[k * rows : (k + 1) * rows] = jnp.concatenate([high, low], axis=1)
        taps = gaussian(row_minus_col((2 * LANES, LANES)) - HALF, sigma, PSF_REACH, scale)
        g_cols[2 * k * LANES : 2 * (k + 1) * LANES] = taps.astype(BF16)

    args = args_ref[...]
    named, weight = args[0:1], weight_ref[...]
    col_values, row_values, factor_values, column, row = slot_tables(
        named, args[1:3], args[3:6], weight, owners, capacity
    )
    source_row[...] = row
    source_copy = pltpu.make_async_copy(source_row, source, source_sem)
    source_copy.start()
    col_table[...] = col_values
    row_table[...] = row_values
    factor_rows[...] = factor_values
    slot_column[...] = column
    for p in range(owners):
        here = jnp.where(named == p, weight * weight, 0.0)
        w_part[p] = jnp.broadcast_to(jnp.sum(here, axis=1, keepdims=True), (8, LANES))

    def warp_chunk(c, carry):
        load(c).wait()

        def warp(step, carry):
            v = c * chunk + step
            result = column_warp(tiles[v], col_table[pl.ds(v, 1), :])
            for m in range(wide // LANES):
                warped[v, :, m * LANES : (m + 1) * LANES] = result[m * rows : (m + 1) * rows]
            return carry

        return lax.fori_loop(0, chunk, warp, carry, unroll=chunk)

    lax.fori_loop(0, chunks, warp_chunk, 0)
    source_copy.wait()

    pl.semaphore_wait(barrier, 2 * owners - 1)

    def pair_copy(q):
        return pltpu.make_async_remote_copy(
            part.at[q, theirs], pair_in.at[q], pair_send.at[q], pair_recv.at[q],
            device_id={"visit": other}, device_id_type=MESH,
        )

    w_copy = pltpu.make_async_remote_copy(
        w_part, w_pair, w_pair_sems.at[0], w_pair_sems.at[1], device_id={"visit": other}, device_id_type=MESH
    )

    def out_copy(q, slot):
        return pltpu.make_async_remote_copy(
            sums.at[q], arrived.at[slot], send.at[q], recv.at[slot], device_id={"patch": q}, device_id_type=MESH
        )

    def w_out_copy(q, slot):
        return pltpu.make_async_remote_copy(
            w_sums.at[q], w_arrived.at[slot], w_send.at[q], w_recv.at[slot], device_id={"patch": q}, device_id_type=MESH
        )

    w_copy.start()

    depth = capacity * rows
    pieces = [(a, min(a + 2 * LANES, wide)) for a in range(0, wide, 2 * LANES)]

    lefts, blurs = (left_even, left_odd), (blur_even, blur_odd)

    def owner(i):
        return (me + i) % owners

    def prepare(i, parity):
        p = owner(i)
        lane_slot = p * capacity + lax.broadcasted_iota(jnp.int32, (count, depth), 1) // rows
        spread = jnp.where(slot_column[...] == lane_slot, 1.0, 0.0).astype(BF16)
        factors = jnp.dot(factor_rows[...], spread, preferred_element_type=F32)
        table_rows = [row_table[pl.ds(p * capacity + r, 1), :] for r in range(capacity)]
        lefts[parity][...] = row_matrices(table_rows, factors, g_rows[...], rows)

    def stack(i, parity):
        p = owner(i)
        slots = [jnp.clip(source[0, p * capacity + r], 0, count - 1) for r in range(capacity)]
        for a, b in pieces:
            right = jnp.concatenate([warped[s, :, a:b] for s in slots], axis=0)
            total = jnp.dot(lefts[parity][...], right, preferred_element_type=F32)
            lane = a + lax.broadcasted_iota(jnp.int32, total.shape, 1)
            if a < HALF or b > wide - HALF:
                total = jnp.where((lane >= HALF) & (lane < wide - HALF), total, 0.0)
            blurs[parity][:, a:b] = total.astype(BF16)

    def match(i, parity):
        p, blur = owner(i), blurs[parity]
        windows = jnp.concatenate(
            [
                jnp.concatenate([blur[k * rows : (k + 1) * rows, m * LANES : (m + 2) * LANES] for k in range(3)], axis=1)
                for m in range(cols // LANES)
            ],
            axis=0,
        )
        result = jnp.dot(windows, g_cols[...], preferred_element_type=F32).astype(BF16)
        for m in range(cols // LANES):
            part[p, :, m * LANES : (m + 1) * LANES] = result[m * rows : (m + 1) * rows]

    def forward(q):
        pair_copy(q).wait()
        sums[q] = (part[q, mine].astype(F32) + pair_in[q].astype(F32)).astype(BF16)
        out_copy(q, me).start()
        w_out_copy(q, me).start()

    prepare(1, 1)
    prepare(2, 0)
    stack(1, 1)
    w_copy.wait()
    w_sums[...] = w_part[...] + w_pair[...]

    def step(i, parity, last=False):
        if not last:
            prepare(i + 1, 1 - parity)
        match(i - 1, 1 - parity)
        pair_copy(owner(i - 1)).start()
        stack(i, parity)
        forward(owner(i - 1))

    def two_patches(j, carry):
        step(2 * j, 0)
        step(2 * j + 1, 1)
        return carry

    lax.fori_loop(1, owners // 2, two_patches, 0)
    step(owners, 0, last=True)
    match(owners, 0)
    pair_copy(me).start()
    pair_copy(me).wait()
    total = part[me, mine].astype(F32) + pair_in[me].astype(F32)

    def collect(i, carry):
        total, weight = carry
        q = (me + owners - i) % owners
        out_copy(q, q).wait_recv()
        w_out_copy(q, q).wait_recv()
        return total + arrived[q].astype(F32), weight + w_arrived[q]

    total, weight = lax.fori_loop(1, owners, collect, (total, w_sums[me]))
    coadd_ref[mine] = total / jnp.sqrt(weight[0:1, 0:1])

    last = pltpu.make_async_remote_copy(
        coadd_ref.at[mine], coadd_ref.at[mine], last_sems.at[0], last_sems.at[1],
        device_id={"visit": other}, device_id_type=MESH,
    )
    last.start()
    neighbour = (me + owners - 1 + 2 * core) % owners
    border = pl.ds(core * (rows - HALO), HALO)

    def halo_copy(to):
        return pltpu.make_async_remote_copy(
            coadd_ref.at[border], halos.at[other], halo_send.at[to], halo_recv.at[other],
            device_id={"patch": neighbour, "visit": to}, device_id_type=MESH,
        )

    for to in range(2):
        halo_copy(to).start()

    def finish(i, carry):
        q = (me + i) % owners
        out_copy(q, me).wait_send()
        w_out_copy(q, me).wait_send()
        return carry

    lax.fori_loop(1, owners, finish, 0)
    for to in range(2):
        halo_copy(to).wait_send()
    for side in range(2):
        pltpu.make_async_remote_copy(
            coadd_ref.at[border], halos.at[side], halo_send.at[0], halo_recv.at[side],
            device_id={"patch": neighbour, "visit": other}, device_id_type=MESH,
        ).wait_recv()
    last.wait()
    before = jnp.where(me > 0, halos[0], 0.0)
    after = jnp.where(me < owners - 1, halos[1], 0.0)
    out_ref[1] = detect(coadd_ref[...], before, after)


def shards(visit_tiles, tile_patch, offsets, psf_coefs, weights):
    count, rows, cols = visit_tiles.shape
    owners = lax.axis_size("patch")
    capacity = max(2, 2 * count // owners)
    capacity += capacity % 2
    chunk = math.gcd(count, 8)
    wide = cols + LANES
    half = rows // 2
    args, first = jnp.zeros((8, count), jnp.int32), 0
    for array in (tile_patch[None, :], offsets.T, psf_coefs.T):
        last = first + array.shape[0]
        args = args + jnp.pad(array, ((first, 8 - last), (0, 0)))
        first = last
    vmem = pl.BlockSpec(memory_space=pltpu.VMEM)
    hbm = pl.BlockSpec(memory_space=pltpu.HBM)
    dma = pltpu.SemaphoreType.DMA
    both = pl.pallas_call(
        functools.partial(fused_kernel, owners, capacity, chunk),
        out_shape=jax.ShapeDtypeStruct((2, rows, cols), F32),
        in_specs=[hbm, vmem, vmem],
        out_specs=vmem,
        scratch_shapes=[
            pltpu.VMEM((count, rows, cols), BF16),
            pltpu.VMEM((count, rows, wide), BF16),
            pltpu.VMEM((3 * rows, wide), BF16),
            pltpu.VMEM((3 * rows, wide), BF16),
            pltpu.VMEM((3 * rows, capacity * rows), BF16),
            pltpu.VMEM((3 * rows, capacity * rows), BF16),
            pltpu.VMEM((owners, rows, cols), BF16),
            pltpu.VMEM((3 * rows, 2 * rows), BF16),
            pltpu.VMEM((6 * LANES, LANES), BF16),
            dma((count // chunk,)),
            pltpu.VMEM((count, LANES), F32),
            pltpu.VMEM((owners * capacity, LANES), F32),
            pltpu.VMEM((8, count), BF16),
            pltpu.VMEM((count, 1), jnp.int32),
            pltpu.VMEM((owners, 8, LANES), F32),
            pltpu.VMEM((1, owners * capacity), jnp.int32),
            pltpu.SMEM((1, owners * capacity), jnp.int32),
            dma(()),
            pltpu.VMEM((owners, half, cols), BF16),
            pltpu.VMEM((owners, half, cols), BF16),
            pltpu.VMEM((owners, half, cols), BF16),
            pltpu.VMEM((owners, 8, LANES), F32),
            pltpu.VMEM((owners, 8, LANES), F32),
            pltpu.VMEM((owners, 8, LANES), F32),
            pltpu.VMEM((2, HALO, cols), F32),
            dma((owners,)), dma((owners,)), dma((2,)),
            dma((owners,)), dma((owners,)), dma((owners,)), dma((owners,)),
            dma((2,)), dma((2,)), dma((2,)),
        ],
        compiler_params=pltpu.CompilerParams(
            collective_id=0, has_side_effects=True, vmem_limit_bytes=52 * 2**20
        ),
        name="fused",
    )(visit_tiles, args, weights.astype(F32)[None, :])
    return both[0], both[1]


def solution(mesh):
    placed = (
        P(("groups", "patch", "visit"), None, None),
        P(("groups", "patch", "visit")),
        P(("groups", "patch", "visit"), None),
        P(("groups", "patch", "visit"), None),
        P(("groups", "patch", "visit")),
    )
    return jax.shard_map(
        shards,
        mesh=mesh,
        in_specs=placed,
        out_specs=(P(("groups", "patch"), None), P(("groups", "patch"), None)),
        check_vma=False,
    )
```

```python
import functools
import math

import jax
import jax.numpy as jnp
import numpy as np
from jax import lax
from jax.experimental import pallas as pl
from jax.experimental.pallas import tpu as pltpu
from jax.sharding import PartitionSpec as P

HALO = 8
PSF_SIGMAS = (0.75, 1.5, 3.0)
PSF_REACH = 16
MID = 5
LANES = 128
HALF = 64
MESH = pl.DeviceIdType.MESH
BF16 = jnp.bfloat16
F32 = jnp.float32


def gaussian_taps(sigma, reach):
    distance = np.arange(-reach, reach + 1, dtype=np.float64)
    return np.exp(-distance * distance / (2.0 * sigma * sigma)) / (math.pi * sigma * sigma) ** 0.25


def well_rounded_scale(sigma, reach):
    taps = gaussian_taps(sigma, reach)
    scales = 1.0 + np.arange(1024) / 1024.0
    scaled = taps[None, :] * scales[:, None]
    rounded = scaled.astype(np.float32).astype(BF16).astype(np.float64)
    error = np.sum((rounded - scaled) ** 2, axis=1) / scales**2
    gain = (np.sum(rounded - scaled, axis=1) / scales) ** 2
    return float(scales[np.argmin(error + gain)])


def gaussian(distance, sigma, reach, scale):
    distance = distance.astype(F32)
    shape = jnp.exp(distance * distance * (-0.5 / (sigma * sigma))) * (scale / (math.pi * sigma * sigma) ** 0.25)
    return jnp.where(jnp.abs(distance) <= reach, shape, 0.0)


def row_minus_col(shape):
    return lax.broadcasted_iota(jnp.int32, shape, 0) - lax.broadcasted_iota(jnp.int32, shape, 1)


def split_high_low(matrix):
    high = matrix.astype(BF16)
    return high, (matrix - high.astype(F32)).astype(BF16)


def sinc(value):
    angle = jnp.where(value == 0.0, 1.0, math.pi * value)
    return jnp.where(value == 0.0, 1.0, jnp.sin(angle) / angle)


def lanczos(value):
    inside = jnp.abs(value) < 3.0
    value = jnp.where(inside, value, 0.0)
    return jnp.where(inside, sinc(value) * sinc(value / 3.0), 0.0)


LOW, HIGH = HALF - 16, HALF + LANES + 16


def column_warp(tile, table_row):
    rows, cols = tile.shape
    shape = (HIGH - LOW, LANES)
    band = pltpu.roll(jnp.broadcast_to(table_row, shape), 0, axis=1, stride=1, stride_axis=0)
    distance = row_minus_col(shape) - (HALF - LOW)
    band = jnp.where(jnp.abs(distance) <= MID, band, 0.0).astype(BF16)
    matrix = jnp.concatenate([jnp.zeros((LOW, LANES), BF16), band, jnp.zeros((2 * LANES - HIGH, LANES), BF16)], axis=0)
    edge = jnp.zeros((rows, LANES), BF16)
    padded = jnp.concatenate([edge, tile, edge], axis=1)
    blocks = cols // LANES + 1
    windows = jnp.concatenate([padded[:, m * LANES : (m + 2) * LANES] for m in range(blocks)], axis=0)
    return jnp.dot(windows, matrix, preferred_element_type=F32).astype(BF16)


def row_matrices(table_rows, factors, g_rows, rows):
    shape = (rows, LANES)
    per = LANES // rows
    lane_slot = lax.broadcasted_iota(jnp.int32, shape, 1) // rows
    shifts = []
    for first in range(0, len(table_rows), per):
        both = jnp.zeros(shape, F32)
        for s in range(per):
            row = jnp.broadcast_to(table_rows[first + s], shape)
            band = pltpu.roll(row, s * rows, axis=1, stride=1, stride_axis=0)
            both = jnp.where(lane_slot == s, band, both)
        shifts.append(both.astype(BF16))
    shift = jnp.concatenate(shifts, axis=1)
    blurred = jnp.dot(g_rows, jnp.concatenate([shift, shift], axis=0), preferred_element_type=F32)
    pieces = []
    for k in range(3):
        factor = factors[k : k + 1, :] + factors[3 + k : 4 + k, :]
        pieces.append(blurred[k * rows : (k + 1) * rows] * factor)
    return jnp.concatenate(pieces, axis=0).astype(BF16)


def detect(coadd, before, after):
    rows, cols = coadd.shape
    sigma = HALO / 4.0
    scale = well_rounded_scale(sigma, HALO)
    extended = jnp.concatenate([before, coadd, after], axis=0)
    h_rows = gaussian(row_minus_col((rows, rows + 2 * HALO)) + HALO, sigma, HALO, 1.0 / scale)
    blurred = jnp.dot(h_rows, extended, preferred_element_type=F32, precision=lax.Precision.HIGHEST).astype(BF16)
    h_cols = gaussian(row_minus_col((3 * LANES, LANES)) - LANES, sigma, HALO, scale).astype(BF16)
    edge = jnp.zeros((rows, LANES), BF16)
    padded = jnp.concatenate([edge, blurred, edge], axis=1)
    windows = jnp.concatenate([padded[:, m * LANES : (m + 3) * LANES] for m in range(cols // LANES)], axis=0)
    result = jnp.dot(windows, h_cols, preferred_element_type=F32)
    return jnp.concatenate([result[m * rows : (m + 1) * rows] for m in range(cols // LANES)], axis=1)


def slot_tables(named, offsets, coefs, weights, owners, capacity):
    count = named.shape[1]
    slots = owners * capacity
    square = (count, count)
    sublane, lane = lax.broadcasted_iota(jnp.int32, square, 0), lax.broadcasted_iota(jnp.int32, square, 1)

    def to_column(row):
        spread = jnp.where(sublane == lane, jnp.broadcast_to(row, square), jnp.zeros(square, row.dtype))
        return jnp.sum(spread, axis=1, keepdims=True)

    named_column = to_column(named)
    same = jnp.where(jnp.broadcast_to(named, square) == jnp.broadcast_to(named_column, square), 1, 0)
    rank_row = jnp.sum(jnp.where(sublane < lane, same, 0), axis=0, keepdims=True)
    rank_column = jnp.sum(jnp.where(lane < sublane, same, 0), axis=1, keepdims=True)
    slot_row = named * capacity + rank_row
    slot_column = named_column * capacity + rank_column

    chosen = lax.broadcasted_iota(jnp.int32, (slots, count), 0) == slot_row
    place = lax.broadcasted_iota(jnp.int32, (count, slots), 1) == slot_column
    tile = lax.broadcasted_iota(jnp.int32, (count, slots), 0)
    source = jnp.sum(jnp.where(place, tile, 0), axis=0, keepdims=True)

    shift = offsets.astype(F32) / 64.0
    at = lax.broadcasted_iota(jnp.int32, (count, LANES), 1)
    col_table = lanczos((at - LANES + HALF - LOW).astype(F32) + to_column(shift[1:2]))
    col_table = col_table.astype(BF16).astype(F32)
    row_table = lanczos(jnp.where(at < HALF, -at, LANES - at).astype(F32) + to_column(shift[0:1]))
    one = jnp.where(chosen, 1.0, 0.0).astype(BF16)
    row_table = jnp.dot(one, row_table.astype(BF16), preferred_element_type=F32)
    factor = weights * (coefs.astype(F32) / 64.0)
    high, low = split_high_low(factor)
    rest = jnp.zeros((2, count), F32)
    factors = jnp.concatenate([high.astype(F32), low.astype(F32), rest], axis=0).astype(BF16)
    return col_table, row_table, factors, slot_column, source


def fused_kernel(
    owners, capacity, chunk,
    tiles_hbm, args_ref, weight_ref,
    out_ref,
    tiles, warped, blur_even, blur_odd, left_even, left_odd, part, g_rows, g_cols, load_sems,
    col_table, row_table, factor_rows, slot_column, w_part, source_row, source, source_sem,
    pair_in, sums, arrived, w_pair, w_sums, w_arrived, halos,
    pair_send, pair_recv, w_pair_sems, send, recv, w_send, w_recv, last_sems, halo_send, halo_recv,
):
    me, core = lax.axis_index("patch"), lax.axis_index("visit")
    other = 1 - core
    count, rows, cols = tiles.shape
    wide = cols + LANES
    half = rows // 2
    chunks = count // chunk
    coadd_ref = out_ref.at[0]
    mine, theirs = pl.ds(core * half, half), pl.ds(other * half, half)

    def load(c):
        span = pl.ds(c * chunk, chunk)
        return pltpu.make_async_copy(tiles_hbm.at[span], tiles.at[span], load_sems.at[c])

    for c in range(chunks):
        load(c).start()

    barrier = pltpu.get_barrier_semaphore()

    def greet(i, carry):
        flat = (me * 2 + core + i) % (2 * owners)
        pl.semaphore_signal(barrier, inc=1, device_id={"patch": flat // 2, "visit": flat % 2}, device_id_type=MESH)
        return carry

    lax.fori_loop(1, 2 * owners, greet, 0)

    for k, sigma in enumerate(PSF_SIGMAS):
        scale = well_rounded_scale(sigma, PSF_REACH)
        high, low = split_high_low(gaussian(row_minus_col((rows, rows)), sigma, PSF_REACH, 1.0 / scale))
        g_rows[k * rows : (k + 1) * rows] = jnp.concatenate([high, low], axis=1)
        taps = gaussian(row_minus_col((2 * LANES, LANES)) - HALF, sigma, PSF_REACH, scale)
        g_cols[2 * k * LANES : 2 * (k + 1) * LANES] = taps.astype(BF16)

    args = args_ref[...]
    named, weight = args[0:1], weight_ref[...]
    col_values, row_values, factor_values, column, row = slot_tables(
        named, args[1:3], args[3:6], weight, owners, capacity
    )
    source_row[...] = row
    source_copy = pltpu.make_async_copy(source_row, source, source_sem)
    source_copy.start()
    col_table[...] = col_values
    row_table[...] = row_values
    factor_rows[...] = factor_values
    slot_column[...] = column
    for p in range(owners):
        here = jnp.where(named == p, weight * weight, 0.0)
        w_part[p] = jnp.broadcast_to(jnp.sum(here, axis=1, keepdims=True), (8, LANES))

    def warp_chunk(c, carry):
        load(c).wait()

        def warp(step, carry):
            v = c * chunk + step
            result = column_warp(tiles[v], col_table[pl.ds(v, 1), :])
            for m in range(wide // LANES):
                warped[v, :, m * LANES : (m + 1) * LANES] = result[m * rows : (m + 1) * rows]
            return carry

        return lax.fori_loop(0, chunk, warp, carry, unroll=chunk)

    lax.fori_loop(0, chunks, warp_chunk, 0)
    source_copy.wait()

    pl.semaphore_wait(barrier, 2 * owners - 1)

    def pair_copy(q):
        return pltpu.make_async_remote_copy(
            part.at[q, theirs], pair_in.at[q], pair_send.at[q], pair_recv.at[q],
            device_id={"visit": other}, device_id_type=MESH,
        )

    w_copy = pltpu.make_async_remote_copy(
        w_part, w_pair, w_pair_sems.at[0], w_pair_sems.at[1], device_id={"visit": other}, device_id_type=MESH
    )

    def out_copy(q, slot):
        return pltpu.make_async_remote_copy(
            sums.at[q], arrived.at[slot], send.at[q], recv.at[slot], device_id={"patch": q}, device_id_type=MESH
        )

    def w_out_copy(q, slot):
        return pltpu.make_async_remote_copy(
            w_sums.at[q], w_arrived.at[slot], w_send.at[q], w_recv.at[slot], device_id={"patch": q}, device_id_type=MESH
        )

    w_copy.start()

    depth = capacity * rows
    pieces = [(a, min(a + 2 * LANES, wide)) for a in range(0, wide, 2 * LANES)]

    lefts, blurs = (left_even, left_odd), (blur_even, blur_odd)

    def owner(i):
        return (me + i) % owners

    def prepare(i, parity):
        p = owner(i)
        lane_slot = p * capacity + lax.broadcasted_iota(jnp.int32, (count, depth), 1) // rows
        spread = jnp.where(slot_column[...] == lane_slot, 1.0, 0.0).astype(BF16)
        factors = jnp.dot(factor_rows[...], spread, preferred_element_type=F32)
        table_rows = [row_table[pl.ds(p * capacity + r, 1), :] for r in range(capacity)]
        lefts[parity][...] = row_matrices(table_rows, factors, g_rows[...], rows)

    def stack(i, parity):
        p = owner(i)
        slots = [jnp.clip(source[0, p * capacity + r], 0, count - 1) for r in range(capacity)]
        for a, b in pieces:
            right = jnp.concatenate([warped[s, :, a:b] for s in slots], axis=0)
            total = jnp.dot(lefts[parity][...], right, preferred_element_type=F32)
            lane = a + lax.broadcasted_iota(jnp.int32, total.shape, 1)
            if a < HALF or b > wide - HALF:
                total = jnp.where((lane >= HALF) & (lane < wide - HALF), total, 0.0)
            blurs[parity][:, a:b] = total.astype(BF16)

    def match(i, parity):
        p, blur = owner(i), blurs[parity]
        windows = jnp.concatenate(
            [
                jnp.concatenate([blur[k * rows : (k + 1) * rows, m * LANES : (m + 2) * LANES] for k in range(3)], axis=1)
                for m in range(cols // LANES)
            ],
            axis=0,
        )
        result = jnp.dot(windows, g_cols[...], preferred_element_type=F32).astype(BF16)
        for m in range(cols // LANES):
            part[p, :, m * LANES : (m + 1) * LANES] = result[m * rows : (m + 1) * rows]

    def forward(q):
        pair_copy(q).wait()
        sums[q] = (part[q, mine].astype(F32) + pair_in[q].astype(F32)).astype(BF16)
        out_copy(q, me).start()
        w_out_copy(q, me).start()

    prepare(1, 1)
    prepare(2, 0)
    stack(1, 1)
    w_copy.wait()
    w_sums[...] = w_part[...] + w_pair[...]

    def step(i, parity, last=False):
        if not last:
            prepare(i + 1, 1 - parity)
        match(i - 1, 1 - parity)
        stack(i, parity)
        pair_copy(owner(i - 1)).start()

    step(2, 0)

    def two_patches(j, carry):
        step(2 * j + 1, 1)
        forward(owner(2 * j - 1))
        step(2 * j + 2, 0)
        forward(owner(2 * j))
        return carry

    lax.fori_loop(1, owners // 2 - 1, two_patches, 0)
    step(owners - 1, 1)
    forward(owner(owners - 3))
    step(owners, 0, last=True)
    forward(owner(owners - 2))
    match(owners, 0)
    pair_copy(me).start()
    forward(owner(owners - 1))
    pair_copy(me).wait()
    total = part[me, mine].astype(F32) + pair_in[me].astype(F32)

    def collect(i, carry):
        total, weight = carry
        q = (me + owners - i) % owners
        out_copy(q, q).wait_recv()
        w_out_copy(q, q).wait_recv()
        return total + arrived[q].astype(F32), weight + w_arrived[q]

    total, weight = lax.fori_loop(1, owners, collect, (total, w_sums[me]))
    coadd_ref[mine] = total / jnp.sqrt(weight[0:1, 0:1])

    last = pltpu.make_async_remote_copy(
        coadd_ref.at[mine], coadd_ref.at[mine], last_sems.at[0], last_sems.at[1],
        device_id={"visit": other}, device_id_type=MESH,
    )
    last.start()
    neighbour = (me + owners - 1 + 2 * core) % owners
    border = pl.ds(core * (rows - HALO), HALO)

    def halo_copy(to):
        return pltpu.make_async_remote_copy(
            coadd_ref.at[border], halos.at[other], halo_send.at[to], halo_recv.at[other],
            device_id={"patch": neighbour, "visit": to}, device_id_type=MESH,
        )

    for to in range(2):
        halo_copy(to).start()

    def finish(i, carry):
        q = (me + i) % owners
        out_copy(q, me).wait_send()
        w_out_copy(q, me).wait_send()
        return carry

    lax.fori_loop(1, owners, finish, 0)
    for to in range(2):
        halo_copy(to).wait_send()
    for side in range(2):
        pltpu.make_async_remote_copy(
            coadd_ref.at[border], halos.at[side], halo_send.at[0], halo_recv.at[side],
            device_id={"patch": neighbour, "visit": other}, device_id_type=MESH,
        ).wait_recv()
    last.wait()
    before = jnp.where(me > 0, halos[0], 0.0)
    after = jnp.where(me < owners - 1, halos[1], 0.0)
    out_ref[1] = detect(coadd_ref[...], before, after)


def shards(visit_tiles, tile_patch, offsets, psf_coefs, weights):
    count, rows, cols = visit_tiles.shape
    owners = lax.axis_size("patch")
    capacity = max(2, 2 * count // owners)
    capacity += capacity % 2
    chunk = math.gcd(count, 8)
    wide = cols + LANES
    half = rows // 2
    args, first = jnp.zeros((8, count), jnp.int32), 0
    for array in (tile_patch[None, :], offsets.T, psf_coefs.T):
        last = first + array.shape[0]
        args = args + jnp.pad(array, ((first, 8 - last), (0, 0)))
        first = last
    vmem = pl.BlockSpec(memory_space=pltpu.VMEM)
    hbm = pl.BlockSpec(memory_space=pltpu.HBM)
    dma = pltpu.SemaphoreType.DMA
    both = pl.pallas_call(
        functools.partial(fused_kernel, owners, capacity, chunk),
        out_shape=jax.ShapeDtypeStruct((2, rows, cols), F32),
        in_specs=[hbm, vmem, vmem],
        out_specs=vmem,
        scratch_shapes=[
            pltpu.VMEM((count, rows, cols), BF16),
            pltpu.VMEM((count, rows, wide), BF16),
            pltpu.VMEM((3 * rows, wide), BF16),
            pltpu.VMEM((3 * rows, wide), BF16),
            pltpu.VMEM((3 * rows, capacity * rows), BF16),
            pltpu.VMEM((3 * rows, capacity * rows), BF16),
            pltpu.VMEM((owners, rows, cols), BF16),
            pltpu.VMEM((3 * rows, 2 * rows), BF16),
            pltpu.VMEM((6 * LANES, LANES), BF16),
            dma((count // chunk,)),
            pltpu.VMEM((count, LANES), F32),
            pltpu.VMEM((owners * capacity, LANES), F32),
            pltpu.VMEM((8, count), BF16),
            pltpu.VMEM((count, 1), jnp.int32),
            pltpu.VMEM((owners, 8, LANES), F32),
            pltpu.VMEM((1, owners * capacity), jnp.int32),
            pltpu.SMEM((1, owners * capacity), jnp.int32),
            dma(()),
            pltpu.VMEM((owners, half, cols), BF16),
            pltpu.VMEM((owners, half, cols), BF16),
            pltpu.VMEM((owners, half, cols), BF16),
            pltpu.VMEM((owners, 8, LANES), F32),
            pltpu.VMEM((owners, 8, LANES), F32),
            pltpu.VMEM((owners, 8, LANES), F32),
            pltpu.VMEM((2, HALO, cols), F32),
            dma((owners,)), dma((owners,)), dma((2,)),
            dma((owners,)), dma((owners,)), dma((owners,)), dma((owners,)),
            dma((2,)), dma((2,)), dma((2,)),
        ],
        compiler_params=pltpu.CompilerParams(
            collective_id=0, has_side_effects=True, vmem_limit_bytes=52 * 2**20
        ),
        name="fused",
    )(visit_tiles, args, weights.astype(F32)[None, :])
    return both[0], both[1]


def solution(mesh):
    placed = (
        P(("groups", "patch", "visit"), None, None),
        P(("groups", "patch", "visit")),
        P(("groups", "patch", "visit"), None),
        P(("groups", "patch", "visit"), None),
        P(("groups", "patch", "visit")),
    )
    return jax.shard_map(
        shards,
        mesh=mesh,
        in_specs=placed,
        out_specs=(P(("groups", "patch"), None), P(("groups", "patch"), None)),
        check_vma=False,
    )
```
